32 devices in a mesh: row: 8 (over y, x, core), col: 4 (over z).
Axes of the slice: x: 2, y: 2, z: 4, core: 2. Of those that a mesh axis runs over, the one named last changes fastest.
Arguments:
- grad: bfloat16 [1152, 128, 128], P(('row', 'col')), may hold values from -6 to 6
- error: float32 [1152, 128, 128], P(('row', 'col')), may hold values from -4 to 4
- sel_blocks: int32 [32, 2], P(('row', 'col')), may hold values from 0 to 36, as said below
- row_bounds: int32 [9], replicated, may hold values from 0 to 12, as said below
- col_bounds: int32 [5], replicated, may hold values from 0 to 3, as said below
- master: float32 [64, 128, 128], P(('row', 'col')), may hold values from -6 to 6
- moment1: float32 [64, 128, 128], P(('row', 'col')), may hold values from -0.06 to 0.06
- moment2: float32 [64, 128, 128], P(('row', 'col')), may hold values from 1e-05 to 0.001
Outputs:
- error_out: float32 [1152, 128, 128], P(('row', 'col'))
- master_out: float32 [64, 128, 128], P(('row', 'col'))
- moment1_out: float32 [64, 128, 128], P(('row', 'col'))
- moment2_out: float32 [64, 128, 128], P(('row', 'col'))
- step_blocks: bfloat16 [36, 128, 128], replicated
The draws below stay inside these ranges and needn't reach their ends.
Inputs may be any that keep to these rules, and one draw needn't show every extreme that they name: `sel_blocks`: each row lists distinct block numbers below 36, then pads with 36; some row lists 2 blocks. `row_bounds`: starts at 0, never falls, ends at 12; a band holds 1 to 2 block rows and some band holds 2. `col_bounds`: starts at 0, never falls, ends at 3; a band holds 0 to 1 block columns and some band holds 1.
All inputs are finite; a program needn't handle non-finite values.
Results may differ from the reference program's by a relative error of at most 0.001.
Values may be sent and summed in bfloat16 or wider, within the bound.
A program may use at most 128 MiB of HBM per device.

```python
import math
import jax
import jax.numpy as jnp
from jax import lax

BS = 128
CMAX = 1
GC = 3
TILE_NUMBER = 36
SEL = 2
OWNCAP = 2
N_ROW = 8
N_COL = 4


def band_starts(key, bands, raised, lowered):
    order = jax.random.permutation(key, bands)
    shifts = jnp.zeros((bands,), jnp.int32).at[order[:raised]].add(1).at[order[raised:raised + lowered]].add(-1)
    band_sizes = 1 + shifts
    return jnp.concatenate([jnp.zeros((1,), jnp.int32), jnp.cumsum(band_sizes).astype(jnp.int32)])


def draw_row_bounds(key, part):
    key = jax.random.fold_in(key, 21)
    return band_starts(key, N_ROW, N_ROW // 2, 0)


def draw_col_bounds(key, part):
    key = jax.random.fold_in(key, 37)
    return band_starts(key, N_COL, 0, N_COL // 4)


def draw_sel_blocks(key, part):
    key = jax.random.fold_in(key, 11)
    worker_sequence = N_ROW * N_COL
    favored_random_seed, rating_random_seed, extra_random_seed, tally_random_seed, entire_random_seed = jax.random.split(key, 5)
    favored_tiles = jax.random.randint(favored_random_seed, (TILE_NUMBER,), 0, 2)
    tile_ranking = jax.random.randint(rating_random_seed, (worker_sequence, TILE_NUMBER), 0, 1024)
    tile_ranking = tile_ranking + 1024 * favored_tiles[None, :] * jax.random.randint(extra_random_seed, (worker_sequence, TILE_NUMBER), 0, 2)
    tile_ranking = tile_ranking * TILE_NUMBER + jnp.arange(TILE_NUMBER, dtype=jnp.int32)[None, :]
    ignored, picked = lax.top_k(tile_ranking, SEL)
    counts = jax.random.randint(tally_random_seed, (worker_sequence,), 1, SEL + 1)
    fullest = jax.random.randint(entire_random_seed, (), 0, worker_sequence)
    counts = jnp.where(jnp.arange(worker_sequence) == fullest, SEL, counts)
    keep = jnp.arange(SEL)[None, :] < counts[:, None]
    return jnp.where(keep, picked, TILE_NUMBER).astype(jnp.int32)


def levels(own_key, shape, cuts, smallest, largest):
    level, own = 1.0, jax.random.fold_in(own_key, 6)
    for dim, shards_of in cuts:
        draws = jnp.exp(jax.random.uniform(jax.random.fold_in(own, dim), (shards_of,), jnp.float32, smallest / len(cuts), largest / len(cuts)))
        level = level * jnp.repeat(draws, shape[dim] // shards_of).reshape([-1 if axis == dim else 1 for axis in range(len(shape))])
    return level


def gaussian(stream_key, extent, deviation, bound, cuts=(), kind=jnp.bfloat16):
    gain = levels(stream_key, extent, cuts, -0.22, 0.18) if cuts else 1.0
    entries = jax.random.normal(stream_key, extent, jnp.float32) * deviation * gain
    return jnp.minimum(jnp.maximum(entries, -bound), bound).astype(kind)


def setup_inputs(seed: int = 0) -> dict:
    seeds = jax.random.split(jax.random.key(seed), 9)
    grad = gaussian(seeds[0], (N_ROW * N_COL * TILE_NUMBER, BS, BS), 1.0, 6.0, ((0, 32),))
    error = gaussian(seeds[1], (N_ROW * N_COL * TILE_NUMBER, BS, BS), 0.5, 4.0, ((0, 32),), jnp.float32)
    sel_blocks = draw_sel_blocks(jax.random.fold_in(seeds[8], 71), 0)
    row_bounds = draw_row_bounds(jax.random.fold_in(seeds[8], 71), 0)
    col_bounds = draw_col_bounds(jax.random.fold_in(seeds[8], 71), 0)
    master = gaussian(seeds[5], (N_ROW * N_COL * OWNCAP, BS, BS), 1.0, 6.0, ((0, 32),), jnp.float32)
    moment1 = gaussian(seeds[6], (N_ROW * N_COL * OWNCAP, BS, BS), 0.01, 0.06, ((0, 32),), jnp.float32)
    moment2 = jnp.clip(jnp.exp(math.log(0.001) - 4.6051703 * jax.random.uniform(seeds[7], (N_ROW * N_COL * OWNCAP, BS, BS), jnp.float32) ** levels(seeds[7], (N_ROW * N_COL * OWNCAP, BS, BS), ((0, 32),), -0.2, 0.2)), 9.999999747378752e-06, 0.001)
    return dict(grad=grad, error=error, sel_blocks=sel_blocks, row_bounds=row_bounds, col_bounds=col_bounds, master=master, moment1=moment1, moment2=moment2)


BETA_ONE = 0.9
BETA_TWO = 0.95
EPSILON = 1e-08
DECAY_RATE = 0.1
LEARN_RATE = 0.01
CORRECT_ONE = 1.0 - 0.9 ** 10
CORRECT_TWO = 1.0 - 0.95 ** 10

def band_of(bounds, positions):
    inner_cuts = bounds[1:-1]
    return lax.optimization_barrier(jnp.sum((inner_cuts[None, :] <= positions[:, None]).astype(jnp.int32), axis=1))

def adamw_update(totals, master, moment1, moment2, worker_sequence):
    averaged = totals / worker_sequence
    first = BETA_ONE * moment1 + (1.0 - BETA_ONE) * averaged
    second = BETA_TWO * moment2 + (1.0 - BETA_TWO) * averaged * averaged
    direction = first / CORRECT_ONE / (jnp.sqrt(second / CORRECT_TWO) + EPSILON) + DECAY_RATE * master
    return (master - LEARN_RATE * direction, first, second, direction)

def reference(grad, error, sel_blocks, row_bounds, col_bounds, master, moment1, moment2):
    worker_sequence = N_ROW * N_COL
    grads = grad.reshape(worker_sequence, TILE_NUMBER, BS, BS)
    errors = error.reshape(worker_sequence, TILE_NUMBER, BS, BS)
    blocks = jnp.arange(TILE_NUMBER, dtype=jnp.int32)

    def visit_device(carry, inputs):
        totals, tallies = carry
        grad_part, error_part, picked = inputs
        accumulated = grad_part.astype(jnp.float32) + error_part
        chosen = lax.optimization_barrier(jnp.sum((picked[:, None] == blocks[None, :]).astype(jnp.float32), axis=0))
        carry_next = (totals + accumulated * chosen[:, None, None], tallies + chosen)
        return (carry_next, accumulated * (1.0 - chosen)[:, None, None])
    start_carry = (jnp.zeros((TILE_NUMBER, BS, BS), jnp.float32), jnp.zeros((TILE_NUMBER,), jnp.float32))
    (totals, tallies), residuals = lax.scan(visit_device, start_carry, (grads, errors, sel_blocks))
    error_out = residuals.reshape(worker_sequence * TILE_NUMBER, BS, BS)
    slot_ids = jnp.arange(worker_sequence * OWNCAP, dtype=jnp.int32)
    owner_of = slot_ids // OWNCAP
    offset_in = slot_ids % OWNCAP
    band_row = owner_of // N_COL
    band_col = owner_of % N_COL
    grid_row = row_bounds[band_row] + offset_in // CMAX
    grid_col = col_bounds[band_col] + offset_in % CMAX
    inside = (grid_row < row_bounds[band_row + 1]) & (grid_col < col_bounds[band_col + 1])
    target = jnp.where(inside, grid_row * GC + grid_col, 0)
    gathered = totals[target]
    counted = tallies[target]
    changed = inside & (counted > 0.5)
    new_master, first, second, direction = adamw_update(gathered, master, moment1, moment2, worker_sequence)
    flags = changed[:, None, None]
    master_out = jnp.where(flags, new_master, master)
    moment1_out = jnp.where(flags, first, moment1)
    moment2_out = jnp.where(flags, second, moment2)
    step_slots = jnp.where(flags, direction, 0.0).astype(jnp.bfloat16)
    block_row = blocks // GC
    block_col = blocks % GC
    row_band = band_of(row_bounds, block_row)
    col_band = band_of(col_bounds, block_col)
    slot_of = (row_band * N_COL + col_band) * OWNCAP + (block_row - row_bounds[row_band]) * CMAX + (block_col - col_bounds[col_band])
    step_blocks = step_slots[slot_of]
    return (error_out, master_out, moment1_out, moment2_out, step_blocks)
```

```python
import functools

import jax
import jax.numpy as jnp
from jax import lax
from jax.experimental import pallas as pl
from jax.experimental.pallas import tpu as pltpu
from jax.sharding import PartitionSpec as P

CMAX = 1
BETA_ONE = 0.9
BETA_TWO = 0.95
EPSILON = 1e-08
DECAY_RATE = 0.1
LEARN_RATE = 0.01
CORRECT_ONE = 1.0 - 0.9**10
CORRECT_TWO = 1.0 - 0.95**10
MESH = pl.DeviceIdType.MESH


def rows_of(start, size, stride):
    return pl.ds(start, size) if stride == 1 else pl.ds(start, size, stride=stride)


def kernel(
    nr, nc, rows, pad,
    sel, rb, cb, grad, error, master, moment1, moment2,
    error_out, master_out, moment1_out, moment2_out, step_out,
    grad_v, err_v, mas_v, mo1_v, mo2_v, acc_v, sums_v,
    id_mine, ids, send1, recv1, onehot, send2, recv2, around, step_v,
    local_sem, out_sem, many_sem, hop_sem, hop_send,
):
    n = nr * nc
    blocks, side = grad.shape[0], grad.shape[1]
    picks, own = sel.shape[1], master.shape[0]
    grid_cols = nc - nc // 4
    r, c = lax.axis_index("row"), lax.axis_index("col")
    me = r * nc + c

    def others(body):
        def step(k, carry):
            to = lax.rem(me + k, n)
            body(to, (to // nc, lax.rem(to, nc)))
            return carry
        lax.fori_loop(1, n, step, 0)

    barrier = pltpu.get_barrier_semaphore()
    loads = [
        pltpu.make_async_copy(a, b, local_sem.at[i])
        for i, (a, b) in enumerate(
            ((grad, grad_v), (error, err_v), (master, mas_v), (moment1, mo1_v), (moment2, mo2_v))
        )
    ]
    for load in loads:
        load.start()
    others(lambda to, where: pl.semaphore_signal(barrier, inc=1, device_id=where, device_id_type=MESH))

    lane = lax.broadcasted_iota(jnp.int32, (1, 128), 1)
    part = lane % pad
    mine = jnp.full((1, 128), -1, jnp.int32)
    for s in range(picks):
        mine = jnp.where(part // rows == s, sel[0, s] * rows + part % rows, mine)
    id_mine[...] = mine
    ids[pl.ds(me, 1)] = mine[None]
    pl.semaphore_wait(barrier, n - 1)

    def send_ids(to, where):
        pltpu.make_async_remote_copy(
            src_ref=id_mine, dst_ref=ids.at[me], send_sem=many_sem.at[0], recv_sem=many_sem.at[1],
            device_id=where, device_id_type=MESH,
        ).start()

    others(send_ids)

    loads[0].wait()
    loads[1].wait()
    if pad > picks * rows:
        send1[...] = jnp.zeros_like(send1)
    for s in range(picks):
        pick = jnp.clip(sel[0, s], 0, blocks - 1)
        acc_v[...] = grad_v[pick].astype(jnp.float32) + err_v[pick]
        for q in range(rows):
            send1[rows_of(s * rows + q, n, pad), :] = acc_v[rows_of(q, n, rows), :]
    recv1[pl.ds(pl.multiple_of(me * pad, pad), pad), :] = send1[pl.ds(pl.multiple_of(me * pad, pad), pad), :]

    def send_stripes(to, where):
        pltpu.make_async_remote_copy(
            src_ref=send1.at[pl.ds(pl.multiple_of(to * pad, pad), pad)],
            dst_ref=recv1.at[pl.ds(pl.multiple_of(me * pad, pad), pad)],
            send_sem=many_sem.at[2], recv_sem=many_sem.at[3],
            device_id=where, device_id_type=MESH,
        ).start()

    others(send_stripes)

    def clear(b, carry):
        chosen = (sel[0, 0] == b).astype(jnp.float32)
        for s in range(1, picks):
            chosen += (sel[0, s] == b).astype(jnp.float32)
        err_v[b] = (grad_v[b].astype(jnp.float32) + err_v[b]) * (1.0 - chosen)
        return carry

    lax.fori_loop(0, blocks, clear, 0)
    keep = pltpu.make_async_copy(err_v, error_out, out_sem.at[0])
    keep.start()

    pltpu.make_async_copy(ids.at[pl.ds(0, n - 1)], ids.at[pl.ds(0, n - 1)], many_sem.at[1]).wait()
    per = 128 // pad
    tiles = []
    for j in range(n * pad // 128):
        tile = jnp.zeros((1, 128), jnp.int32)
        for k in range(per):
            tile = jnp.where(lane // pad == k, ids[j * per + k], tile)
        tiles.append(jnp.broadcast_to(tile, (pad, 128)))
    sub = lax.broadcasted_iota(jnp.int32, (pad, 128), 0)
    slot, inner = sub // rows, sub % rows

    def mark(o, carry):
        band, col_band = o // nc, lax.rem(o, nc)
        grid_row = rb[band] + slot // CMAX
        grid_col = cb[col_band] + slot % CMAX
        inside = (grid_row < rb[band + 1]) & (grid_col < cb[col_band + 1]) & (slot < own)
        wanted = jnp.where(inside, (grid_row * grid_cols + grid_col) * rows + inner, -2)
        for j, tile in enumerate(tiles):
            onehot[pl.ds(pl.multiple_of(o * pad, pad), pad), j * 128:(j + 1) * 128] = (
                wanted == tile
            ).astype(jnp.float32)
        return carry

    lax.fori_loop(0, n, mark, 0)

    pltpu.make_async_copy(
        recv1.at[pl.ds(0, (n - 1) * pad)], recv1.at[pl.ds(0, (n - 1) * pad)], many_sem.at[3]
    ).wait()
    got = recv1[...]
    high = got.astype(jnp.bfloat16)
    rest = got - high.astype(jnp.float32)
    middle = rest.astype(jnp.bfloat16)
    low = (rest - middle.astype(jnp.float32)).astype(jnp.bfloat16)
    table = onehot[...].astype(jnp.bfloat16)
    dot = functools.partial(jnp.dot, preferred_element_type=jnp.float32)
    send2[...] = dot(table, high) + (dot(table, middle) + dot(table, low))
    recv2[pl.ds(pl.multiple_of(me * pad, pad), pad), :] = send2[pl.ds(pl.multiple_of(me * pad, pad), pad), :]

    def send_sums(to, where):
        pltpu.make_async_remote_copy(
            src_ref=send2.at[pl.ds(pl.multiple_of(to * pad, pad), pad)],
            dst_ref=recv2.at[pl.ds(pl.multiple_of(me * pad, pad), pad)],
            send_sem=many_sem.at[4], recv_sem=many_sem.at[5],
            device_id=where, device_id_type=MESH,
        ).start()

    others(send_sums)
    counts = jnp.sum(onehot[pl.ds(pl.multiple_of(me * pad, pad), pad), :], axis=1, keepdims=True)
    for load in loads[2:]:
        load.wait()
    pltpu.make_async_copy(
        recv2.at[pl.ds(0, (n - 1) * pad)], recv2.at[pl.ds(0, (n - 1) * pad)], many_sem.at[5]
    ).wait()

    for s in range(own):
        for q in range(rows):
            sums_v[rows_of(q, n, rows), :] = recv2[rows_of(s * rows + q, n, pad), :]
        changed = jnp.broadcast_to(counts[s * rows:s * rows + 1, :], (side, side)) > 0.5
        averaged = sums_v[...] / n
        old = mas_v[s]
        first = BETA_ONE * mo1_v[s] + (1.0 - BETA_ONE) * averaged
        second = BETA_TWO * mo2_v[s] + (1.0 - BETA_TWO) * averaged * averaged
        direction = (
            first / CORRECT_ONE / (jnp.sqrt(second / CORRECT_TWO) + EPSILON) + DECAY_RATE * old
        )
        around[me * own + s] = jnp.where(changed, direction, 0.0).astype(jnp.bfloat16)
        mas_v[s] = jnp.where(changed, old - LEARN_RATE * direction, old)
        mo1_v[s] = jnp.where(changed, first, mo1_v[s])
        mo2_v[s] = jnp.where(changed, second, mo2_v[s])

    def piece(dev_row, dev_col, half=None):
        start = (dev_row * nc + dev_col) * own
        if half is None:
            return around.at[pl.ds(start, own)]
        return around.at[pl.ds(start + half * (own // 2), own // 2)]

    def hop(ref, kind, index, where):
        pltpu.make_async_remote_copy(
            src_ref=ref, dst_ref=ref, send_sem=hop_send, recv_sem=hop_sem.at[kind, index],
            device_id=where, device_id_type=MESH,
        ).start()

    def landed(ref, kind, index):
        pltpu.make_async_copy(ref, ref, hop_sem.at[kind, index]).wait()

    stores = [
        pltpu.make_async_copy(a, b, out_sem.at[1 + i])
        for i, (a, b) in enumerate(((mas_v, master_out), (mo1_v, moment1_out), (mo2_v, moment2_out)))
    ]
    if nr == 8 and own % 2 == 0:
        near = r + 1 - 2 * lax.rem(r, 2)
        beside = r + 2 - 4 * lax.rem(r // 2, 2)
        across = r + 4 - 8 * lax.rem(r // 4, 2)
        far = beside + 4 - 8 * lax.rem(beside // 4, 2)
        for k in range(1, nc):
            hop(piece(r, c), 0, c, (r, lax.rem(c + k, nc)))

        def spread(z):
            hop(piece(r, z), 1, z, (beside, c))
            hop(piece(r, z), 2, z, (across, c))
            hop(piece(r, z), 5, z, (near, c))

        def relay(z):
            landed(piece(beside, z), 1, z)
            hop(piece(beside, z, 0), 3, z, (across, c))
            hop(piece(beside, z), 6, z, (near, c))
            landed(piece(across, z), 2, z)
            hop(piece(across, z, 1), 4, z, (beside, c))
            hop(piece(across, z), 7, z, (near, c))

        def finish(z):
            landed(piece(far, z, 0), 3, z)
            landed(piece(far, z, 1), 4, z)
            hop(piece(far, z), 8, z, (near, c))

        for k in range(nc + 2):
            if k < nc:
                z = lax.rem(c + k, nc)
                if k:
                    landed(piece(r, z), 0, z)
                spread(z)
                if k == 0:
                    for store in stores:
                        store.start()
            if 1 <= k < nc + 1:
                relay(lax.rem(c + k - 1, nc))
            if k >= 2:
                finish(lax.rem(c + k - 2, nc))
        nears = (near, near + 2 - 4 * lax.rem(near // 2, 2))
        nears = nears + tuple(v + 4 - 8 * lax.rem(v // 4, 2) for v in nears)
        for k in range(nc):
            z = lax.rem(c + k, nc)
            landed(piece(nears[0], z), 5, z)
            landed(piece(nears[1], z), 6, z)
            landed(piece(nears[2], z), 7, z)
            landed(piece(nears[3], z), 8, z)
    else:
        others(lambda to, where: hop(piece(r, c), 0, 0, where))
        for store in stores:
            store.start()
        landed(around.at[pl.ds(0, (n - 1) * own)], 0, 0)

    for b in range(blocks):
        grid_row, grid_col = b // grid_cols, b % grid_cols
        band, col_band = jnp.int32(0), jnp.int32(0)
        for i in range(1, nr):
            band += (rb[i] <= grid_row).astype(jnp.int32)
        for i in range(1, nc):
            col_band += (cb[i] <= grid_col).astype(jnp.int32)
        where = (band * nc + col_band) * own + (grid_row - rb[band]) * CMAX + grid_col - cb[col_band]
        step_v[b] = around[jnp.clip(where, 0, n * own - 1)]
    done = pltpu.make_async_copy(step_v, step_out, out_sem.at[4])
    done.start()

    for i, ref in ((0, ids.at[pl.ds(0, n - 1)]), (2, send1.at[pl.ds(0, (n - 1) * pad)]), (4, send2.at[pl.ds(0, (n - 1) * pad)])):
        pltpu.make_async_copy(ref, ref, many_sem.at[i]).wait()
    landed_all = around.at[pl.ds(0, (n - 1) * own)]
    pltpu.make_async_copy(landed_all, landed_all, hop_send).wait()
    keep.wait()
    for store in stores:
        store.wait()
    done.wait()


def solution(mesh):
    nr, nc = mesh.shape["row"], mesh.shape["col"]
    n = nr * nc

    def local(grad, error, sel_blocks, row_bounds, col_bounds, master, moment1, moment2):
        blocks, side, _ = grad.shape
        picks, own = sel_blocks.shape[1], master.shape[0]
        rows = side // n
        pad = -(-max(picks, own) * rows // 8) * 8
        f32, bf16 = jnp.float32, jnp.bfloat16
        smem = pl.BlockSpec(memory_space=pltpu.SMEM)
        anywhere = pl.BlockSpec(memory_space=pl.ANY)
        slots = jax.ShapeDtypeStruct(master.shape, f32)
        return pl.pallas_call(
            functools.partial(kernel, nr, nc, rows, pad),
            out_shape=(
                jax.ShapeDtypeStruct(error.shape, f32), slots, slots, slots,
                jax.ShapeDtypeStruct(grad.shape, bf16),
            ),
            in_specs=[smem] * 3 + [anywhere] * 5,
            out_specs=[anywhere] * 5,
            scratch_shapes=[
                pltpu.VMEM(grad.shape, bf16),
                pltpu.VMEM(error.shape, f32),
                pltpu.VMEM(master.shape, f32),
                pltpu.VMEM(master.shape, f32),
                pltpu.VMEM(master.shape, f32),
                pltpu.VMEM((side, side), f32),
                pltpu.VMEM((side, side), f32),
                pltpu.VMEM((1, 128), jnp.int32),
                pltpu.VMEM((n, 1, 128), jnp.int32),
                pltpu.VMEM((n * pad, side), f32),
                pltpu.VMEM((n * pad, side), f32),
                pltpu.VMEM((n * pad, n * pad), f32),
                pltpu.VMEM((n * pad, side), f32),
                pltpu.VMEM((n * pad, side), f32),
                pltpu.VMEM((n * own, side, side), bf16),
                pltpu.VMEM(grad.shape, bf16),
                pltpu.SemaphoreType.DMA((5,)),
                pltpu.SemaphoreType.DMA((5,)),
                pltpu.SemaphoreType.DMA((6,)),
                pltpu.SemaphoreType.DMA((9, nc)),
                pltpu.SemaphoreType.DMA,
            ],
            compiler_params=pltpu.CompilerParams(
                collective_id=0, has_side_effects=True, vmem_limit_bytes=48 * 1024 * 1024
            ),
        )(sel_blocks, row_bounds, col_bounds, grad, error, master, moment1, moment2)

    whole = P(("row", "col"), None, None)
    return jax.shard_map(
        local,
        mesh=mesh,
        in_specs=(whole, whole, P(("row", "col"), None), P(), P(), whole, whole, whole),
        out_specs=(whole, whole, whole, whole, P()),
        check_vma=False,
    )
```

```python
import functools

import jax
import jax.numpy as jnp
from jax import lax
from jax.experimental import pallas as pl
from jax.experimental.pallas import tpu as pltpu
from jax.sharding import PartitionSpec as P

CMAX = 1
BETA_ONE = 0.9
BETA_TWO = 0.95
EPSILON = 1e-08
DECAY_RATE = 0.1
LEARN_RATE = 0.01
CORRECT_ONE = 1.0 - 0.9**10
CORRECT_TWO = 1.0 - 0.95**10
MESH = pl.DeviceIdType.MESH


def rows_of(start, size, stride):
    return pl.ds(start, size) if stride == 1 else pl.ds(start, size, stride=stride)


def kernel(
    nr, nc, rows, pad,
    sel_hbm, rb_hbm, cb_hbm, grad, error, master, moment1, moment2,
    error_out, master_out, moment1_out, moment2_out, around,
    sel, rb, cb, grad_v, err_v, mas_v, mo1_v, mo2_v, acc_v, sums_v,
    id_mine, ids, send1, recv1, onehot, send2, recv2, dir_v,
    local_sem, out_sem, many_sem, hop_sem, hop_send,
):
    n = nr * nc
    blocks, side = grad.shape[0], grad.shape[1]
    picks, own = sel.shape[1], master.shape[0]
    grid_cols = nc - nc // 4
    r, c = lax.axis_index("row"), lax.axis_index("col")
    me = r * nc + c

    def others(body):
        def step(k, carry):
            to = lax.rem(me + k, n)
            body(to, (to // nc, lax.rem(to, nc)))
            return carry
        lax.fori_loop(1, n, step, 0)

    barrier = pltpu.get_barrier_semaphore()
    loads = [
        pltpu.make_async_copy(a, b, local_sem.at[i])
        for i, (a, b) in enumerate(
            (
                (grad, grad_v), (error, err_v), (master, mas_v), (moment1, mo1_v), (moment2, mo2_v),
                (sel_hbm, sel), (rb_hbm, rb), (cb_hbm, cb),
            )
        )
    ]
    for load in loads:
        load.start()
    others(lambda to, where: pl.semaphore_signal(barrier, inc=1, device_id=where, device_id_type=MESH))

    for load in loads[5:]:
        load.wait()

    lane = lax.broadcasted_iota(jnp.int32, (1, 128), 1)
    part = lane % pad
    mine = jnp.full((1, 128), -1, jnp.int32)
    for s in range(picks):
        mine = jnp.where(part // rows == s, sel[0, s] * rows + part % rows, mine)
    id_mine[...] = mine
    ids[pl.ds(me, 1)] = mine[None]
    pl.semaphore_wait(barrier, n - 1)

    loads[0].wait()
    loads[1].wait()
    if pad > picks * rows:
        send1[...] = jnp.zeros_like(send1)
    for s in range(picks):
        pick = jnp.clip(sel[0, s], 0, blocks - 1)
        acc_v[...] = grad_v[pick].astype(jnp.float32) + err_v[pick]
        for q in range(rows):
            send1[rows_of(s * rows + q, n, pad), :] = acc_v[rows_of(q, n, rows), :]
    recv1[pl.ds(pl.multiple_of(me * pad, pad), pad), :] = send1[pl.ds(pl.multiple_of(me * pad, pad), pad), :]

    def send_stripes(to, where):
        pltpu.make_async_remote_copy(
            src_ref=send1.at[pl.ds(pl.multiple_of(to * pad, pad), pad)],
            dst_ref=recv1.at[pl.ds(pl.multiple_of(me * pad, pad), pad)],
            send_sem=many_sem.at[2], recv_sem=many_sem.at[3],
            device_id=where, device_id_type=MESH,
        ).start()

    others(send_stripes)

    def send_ids(to, where):
        pltpu.make_async_remote_copy(
            src_ref=id_mine, dst_ref=ids.at[me], send_sem=many_sem.at[0], recv_sem=many_sem.at[1],
            device_id=where, device_id_type=MESH,
        ).start()

    others(send_ids)

    def clear(b, carry):
        chosen = (sel[0, 0] == b).astype(jnp.float32)
        for s in range(1, picks):
            chosen += (sel[0, s] == b).astype(jnp.float32)
        err_v[b] = (grad_v[b].astype(jnp.float32) + err_v[b]) * (1.0 - chosen)
        return carry

    lax.fori_loop(0, blocks, clear, 0)
    keep = pltpu.make_async_copy(err_v, error_out, out_sem.at[0])
    keep.start()

    pltpu.make_async_copy(ids.at[pl.ds(0, n - 1)], ids.at[pl.ds(0, n - 1)], many_sem.at[1]).wait()
    per = 128 // pad
    tiles = []
    for j in range(n * pad // 128):
        tile = jnp.zeros((1, 128), jnp.int32)
        for k in range(per):
            tile = jnp.where(lane // pad == k, ids[j * per + k], tile)
        tiles.append(jnp.broadcast_to(tile, (pad, 128)))
    sub = lax.broadcasted_iota(jnp.int32, (pad, 128), 0)
    slot, inner = sub // rows, sub % rows

    def mark(o, carry):
        band, col_band = o // nc, lax.rem(o, nc)
        grid_row = rb[band] + slot // CMAX
        grid_col = cb[col_band] + slot % CMAX
        inside = (grid_row < rb[band + 1]) & (grid_col < cb[col_band + 1]) & (slot < own)
        wanted = jnp.where(inside, (grid_row * grid_cols + grid_col) * rows + inner, -2)
        for j, tile in enumerate(tiles):
            onehot[pl.ds(pl.multiple_of(o * pad, pad), pad), j * 128:(j + 1) * 128] = (
                wanted == tile
            ).astype(jnp.float32)
        return carry

    lax.fori_loop(0, n, mark, 0)

    pltpu.make_async_copy(
        recv1.at[pl.ds(0, (n - 1) * pad)], recv1.at[pl.ds(0, (n - 1) * pad)], many_sem.at[3]
    ).wait()
    got = recv1[...]
    high = got.astype(jnp.bfloat16)
    rest = got - high.astype(jnp.float32)
    middle = rest.astype(jnp.bfloat16)
    low = (rest - middle.astype(jnp.float32)).astype(jnp.bfloat16)
    table = onehot[...].astype(jnp.bfloat16)
    dot = functools.partial(jnp.dot, preferred_element_type=jnp.float32)
    send2[...] = dot(table, high) + (dot(table, middle) + dot(table, low))
    recv2[pl.ds(pl.multiple_of(me * pad, pad), pad), :] = send2[pl.ds(pl.multiple_of(me * pad, pad), pad), :]

    def send_sums(to, where):
        pltpu.make_async_remote_copy(
            src_ref=send2.at[pl.ds(pl.multiple_of(to * pad, pad), pad)],
            dst_ref=recv2.at[pl.ds(pl.multiple_of(me * pad, pad), pad)],
            send_sem=many_sem.at[4], recv_sem=many_sem.at[5],
            device_id=where, device_id_type=MESH,
        ).start()

    others(send_sums)
    counts = jnp.sum(onehot[pl.ds(pl.multiple_of(me * pad, pad), pad), :], axis=1, keepdims=True)
    for load in loads[2:5]:
        load.wait()
    pltpu.make_async_copy(
        recv2.at[pl.ds(0, (n - 1) * pad)], recv2.at[pl.ds(0, (n - 1) * pad)], many_sem.at[5]
    ).wait()

    for s in range(own):
        for q in range(rows):
            sums_v[rows_of(q, n, rows), :] = recv2[rows_of(s * rows + q, n, pad), :]
        changed = jnp.broadcast_to(counts[s * rows:s * rows + 1, :], (side, side)) > 0.5
        averaged = sums_v[...] / n
        old = mas_v[s]
        first = BETA_ONE * mo1_v[s] + (1.0 - BETA_ONE) * averaged
        second = BETA_TWO * mo2_v[s] + (1.0 - BETA_TWO) * averaged * averaged
        direction = (
            first / CORRECT_ONE / (jnp.sqrt(second / CORRECT_TWO) + EPSILON) + DECAY_RATE * old
        )
        dir_v[s] = jnp.where(changed, direction, 0.0).astype(jnp.bfloat16)
        mas_v[s] = jnp.where(changed, old - LEARN_RATE * direction, old)
        mo1_v[s] = jnp.where(changed, first, mo1_v[s])
        mo2_v[s] = jnp.where(changed, second, mo2_v[s])

    def piece(dev_row, dev_col, half=None):
        start = (dev_row * nc + dev_col) * own
        if half is None:
            return around.at[pl.ds(start, own)]
        return around.at[pl.ds(start + half * (own // 2), own // 2)]

    def hop(ref, kind, index, where, src=None):
        pltpu.make_async_remote_copy(
            src_ref=ref if src is None else src, dst_ref=ref, send_sem=hop_send, recv_sem=hop_sem.at[kind, index],
            device_id=where, device_id_type=MESH,
        ).start()

    def landed(ref, kind, index):
        pltpu.make_async_copy(ref, ref, hop_sem.at[kind, index]).wait()

    own_piece = pltpu.make_async_copy(dir_v, piece(r, c), out_sem.at[4])
    own_piece.start()
    stores = [
        pltpu.make_async_copy(a, b, out_sem.at[1 + i])
        for i, (a, b) in enumerate(((mas_v, master_out), (mo1_v, moment1_out), (mo2_v, moment2_out)))
    ]
    if nr == 8 and own % 2 == 0:
        near = r + 1 - 2 * lax.rem(r, 2)
        beside = r + 2 - 4 * lax.rem(r // 2, 2)
        across = r + 4 - 8 * lax.rem(r // 4, 2)
        far = beside + 4 - 8 * lax.rem(beside // 4, 2)
        for k in range(1, nc):
            hop(piece(r, c), 0, c, (r, lax.rem(c + k, nc)), dir_v)

        def spread(z, src=None):
            hop(piece(r, z), 1, z, (beside, c), src)
            hop(piece(r, z), 2, z, (across, c), src)
            hop(piece(r, z), 5, z, (near, c), src)

        def relay(z):
            landed(piece(beside, z), 1, z)
            hop(piece(beside, z, 0), 3, z, (across, c))
            hop(piece(beside, z), 6, z, (near, c))
            landed(piece(across, z), 2, z)
            hop(piece(across, z, 1), 4, z, (beside, c))
            hop(piece(across, z), 7, z, (near, c))

        def finish(z):
            landed(piece(far, z, 0), 3, z)
            landed(piece(far, z, 1), 4, z)
            hop(piece(far, z), 8, z, (near, c))

        for k in range(nc + 2):
            if k < nc:
                z = lax.rem(c + k, nc)
                if k:
                    landed(piece(r, z), 0, z)
                spread(z, None if k else dir_v)
                if k == 0:
                    for store in stores:
                        store.start()
            if 1 <= k < nc + 1:
                relay(lax.rem(c + k - 1, nc))
            if k >= 2:
                finish(lax.rem(c + k - 2, nc))
        nears = (near, near + 2 - 4 * lax.rem(near // 2, 2))
        nears = nears + tuple(v + 4 - 8 * lax.rem(v // 4, 2) for v in nears)
        for k in range(nc):
            z = lax.rem(c + k, nc)
            landed(piece(nears[0], z), 5, z)
            landed(piece(nears[1], z), 6, z)
            landed(piece(nears[2], z), 7, z)
            landed(piece(nears[3], z), 8, z)
    else:
        others(lambda to, where: hop(piece(r, c), 0, 0, where, dir_v))
        for store in stores:
            store.start()
        landed(around.at[pl.ds(0, (n - 1) * own)], 0, 0)

    for i, ref in ((0, ids.at[pl.ds(0, n - 1)]), (2, send1.at[pl.ds(0, (n - 1) * pad)]), (4, send2.at[pl.ds(0, (n - 1) * pad)])):
        pltpu.make_async_copy(ref, ref, many_sem.at[i]).wait()
    landed_all = around.at[pl.ds(0, (n - 1) * own)]
    pltpu.make_async_copy(landed_all, landed_all, hop_send).wait()
    keep.wait()
    for store in stores:
        store.wait()
    own_piece.wait()


def place(
    nr, nc, rb, cb, error_in, master_in, moment1_in, moment2_in, around,
    error_out, master_out, moment1_out, moment2_out, step_out, sem, step_sem,
):
    blocks, own = step_out.shape[0], master_in.shape[0]
    grid_cols = nc - nc // 4
    copies = [
        pltpu.make_async_copy(a, b, sem.at[i])
        for i, (a, b) in enumerate(
            (
                (error_in, error_out), (master_in, master_out),
                (moment1_in, moment1_out), (moment2_in, moment2_out),
            )
        )
    ]
    for copy in copies:
        copy.start()
    col_of = []
    for grid_col in range(grid_cols):
        band = jnp.int32(0)
        for i in range(1, nc):
            band += (cb[i] <= grid_col).astype(jnp.int32)
        col_of.append(band * own + grid_col - cb[band])
    for grid_row in range(blocks // grid_cols):
        band = jnp.int32(0)
        for i in range(1, nr):
            band += (rb[i] <= grid_row).astype(jnp.int32)
        base = band * nc * own + (grid_row - rb[band]) * CMAX
        for grid_col in range(grid_cols):
            b = grid_row * grid_cols + grid_col
            slot = jnp.clip(base + col_of[grid_col], 0, nr * nc * own - 1)
            pltpu.make_async_copy(around.at[slot], step_out.at[b], step_sem).start()
    pltpu.make_async_copy(around.at[pl.ds(0, blocks)], step_out, step_sem).wait()
    for copy in copies:
        copy.wait()


def solution(mesh):
    nr, nc = mesh.shape["row"], mesh.shape["col"]
    n = nr * nc

    def local(grad, error, sel_blocks, row_bounds, col_bounds, master, moment1, moment2):
        blocks, side, _ = grad.shape
        picks, own = sel_blocks.shape[1], master.shape[0]
        rows = side // n
        pad = -(-max(picks, own) * rows // 8) * 8
        f32, bf16 = jnp.float32, jnp.bfloat16
        smem = pl.BlockSpec(memory_space=pltpu.SMEM)
        anywhere = pl.BlockSpec(memory_space=pl.ANY)
        slots = jax.ShapeDtypeStruct(master.shape, f32)
        parts = pl.pallas_call(
            functools.partial(kernel, nr, nc, rows, pad),
            out_shape=(
                jax.ShapeDtypeStruct(error.shape, f32), slots, slots, slots,
                jax.ShapeDtypeStruct((n * own, side, side), bf16),
            ),
            in_specs=[pl.BlockSpec(memory_space=pltpu.HBM)] * 8,
            out_specs=[anywhere] * 5,
            scratch_shapes=[
                pltpu.SMEM(sel_blocks.shape, jnp.int32),
                pltpu.SMEM(row_bounds.shape, jnp.int32),
                pltpu.SMEM(col_bounds.shape, jnp.int32),
                pltpu.VMEM(grad.shape, bf16),
                pltpu.VMEM(error.shape, f32),
                pltpu.VMEM(master.shape, f32),
                pltpu.VMEM(master.shape, f32),
                pltpu.VMEM(master.shape, f32),
                pltpu.VMEM((side, side), f32),
                pltpu.VMEM((side, side), f32),
                pltpu.VMEM((1, 128), jnp.int32),
                pltpu.VMEM((n, 1, 128), jnp.int32),
                pltpu.VMEM((n * pad, side), f32),
                pltpu.VMEM((n * pad, side), f32),
                pltpu.VMEM((n * pad, n * pad), f32),
                pltpu.VMEM((n * pad, side), f32),
                pltpu.VMEM((n * pad, side), f32),
                pltpu.VMEM(master.shape, bf16),
                pltpu.SemaphoreType.DMA((8,)),
                pltpu.SemaphoreType.DMA((5,)),
                pltpu.SemaphoreType.DMA((6,)),
                pltpu.SemaphoreType.DMA((9, nc)),
                pltpu.SemaphoreType.DMA,
            ],
            compiler_params=pltpu.CompilerParams(
                collective_id=0, has_side_effects=True, vmem_limit_bytes=64 * 1024 * 1024
            ),
        )(sel_blocks, row_bounds, col_bounds, grad, error, master, moment1, moment2)
        return pl.pallas_call(
            functools.partial(place, nr, nc),
            out_shape=(
                jax.ShapeDtypeStruct(error.shape, f32), slots, slots, slots,
                jax.ShapeDtypeStruct(grad.shape, bf16),
            ),
            in_specs=[smem] * 2 + [anywhere] * 5,
            out_specs=[pl.BlockSpec(memory_space=pltpu.HBM)] * 5,
            scratch_shapes=[pltpu.SemaphoreType.DMA((4,)), pltpu.SemaphoreType.DMA],
            compiler_params=pltpu.CompilerParams(vmem_limit_bytes=64 * 1024 * 1024),
        )(row_bounds, col_bounds, *parts)

    whole = P(("row", "col"), None, None)
    return jax.shard_map(
        local,
        mesh=mesh,
        in_specs=(whole, whole, P(("row", "col"), None), P(), P(), whole, whole, whole),
        out_specs=(whole, whole, whole, whole, P()),
        check_vma=False,
    )
```

```python
import functools

import jax
import jax.numpy as jnp
from jax import lax
from jax.experimental import pallas as pl
from jax.experimental.pallas import tpu as pltpu
from jax.sharding import PartitionSpec as P

CMAX = 1
BETA_ONE = 0.9
BETA_TWO = 0.95
EPSILON = 1e-08
DECAY_RATE = 0.1
LEARN_RATE = 0.01
CORRECT_ONE = 1.0 - 0.9**10
CORRECT_TWO = 1.0 - 0.95**10
MESH = pl.DeviceIdType.MESH


def rows_of(start, size, stride):
    return pl.ds(start, size) if stride == 1 else pl.ds(start, size, stride=stride)


def kernel(
    nr, nc, rows, pad,
    sel_hbm, rb_hbm, cb_hbm, grad, error, master, moment1, moment2,
    error_out, master_out, moment1_out, moment2_out, around,
    sel, rb, cb, grad_v, err_v, mas_v, mo1_v, mo2_v, acc_v, sums_v,
    id_mine, ids, send1, recv1, onehot, send2, recv2, dir_v,
    local_sem, out_sem, many_sem, hop_sem, hop_send,
):
    n = nr * nc
    blocks, side = grad.shape[0], grad.shape[1]
    picks, own = sel.shape[1], master.shape[0]
    grid_cols = nc - nc // 4
    r, c = lax.axis_index("row"), lax.axis_index("col")
    me = r * nc + c

    def others(body):
        def step(k, carry):
            to = lax.rem(me + k, n)
            body(to, (to // nc, lax.rem(to, nc)))
            return carry
        lax.fori_loop(1, n, step, 0)

    barrier = pltpu.get_barrier_semaphore()
    loads = [
        pltpu.make_async_copy(a, b, local_sem.at[i])
        for i, (a, b) in enumerate(
            (
                (grad, grad_v), (error, err_v), (master, mas_v), (moment1, mo1_v), (moment2, mo2_v),
                (sel_hbm, sel), (rb_hbm, rb), (cb_hbm, cb),
            )
        )
    ]
    for load in loads:
        load.start()
    others(lambda to, where: pl.semaphore_signal(barrier, inc=1, device_id=where, device_id_type=MESH))

    for load in loads[5:]:
        load.wait()

    lane = lax.broadcasted_iota(jnp.int32, (1, 128), 1)
    part = lane % pad
    mine = jnp.full((1, 128), -1, jnp.int32)
    for s in range(picks):
        mine = jnp.where(part // rows == s, sel[0, s] * rows + part % rows, mine)
    id_mine[...] = mine
    ids[pl.ds(me, 1)] = mine[None]
    pl.semaphore_wait(barrier, n - 1)

    loads[0].wait()
    loads[1].wait()
    if pad > picks * rows:
        send1[...] = jnp.zeros_like(send1)
    for s in range(picks):
        pick = jnp.clip(sel[0, s], 0, blocks - 1)
        acc_v[...] = grad_v[pick].astype(jnp.float32) + err_v[pick]
        for q in range(rows):
            send1[rows_of(s * rows + q, n, pad), :] = acc_v[rows_of(q, n, rows), :]
    recv1[pl.ds(pl.multiple_of(me * pad, pad), pad), :] = send1[pl.ds(pl.multiple_of(me * pad, pad), pad), :]

    def send_stripes(to, where):
        pltpu.make_async_remote_copy(
            src_ref=send1.at[pl.ds(pl.multiple_of(to * pad, pad), pad)],
            dst_ref=recv1.at[pl.ds(pl.multiple_of(me * pad, pad), pad)],
            send_sem=many_sem.at[2], recv_sem=many_sem.at[3],
            device_id=where, device_id_type=MESH,
        ).start()

    others(send_stripes)

    def send_ids(to, where):
        pltpu.make_async_remote_copy(
            src_ref=id_mine, dst_ref=ids.at[me], send_sem=many_sem.at[0], recv_sem=many_sem.at[1],
            device_id=where, device_id_type=MESH,
        ).start()

    others(send_ids)

    def clear(b, carry):
        chosen = (sel[0, 0] == b).astype(jnp.float32)
        for s in range(1, picks):
            chosen += (sel[0, s] == b).astype(jnp.float32)
        err_v[b] = (grad_v[b].astype(jnp.float32) + err_v[b]) * (1.0 - chosen)
        return carry

    lax.fori_loop(0, blocks, clear, 0)
    keep = pltpu.make_async_copy(err_v, error_out, out_sem.at[0])
    keep.start()

    pltpu.make_async_copy(ids.at[pl.ds(0, n - 1)], ids.at[pl.ds(0, n - 1)], many_sem.at[1]).wait()
    per = 128 // pad
    tiles = []
    for j in range(n * pad // 128):
        tile = jnp.zeros((1, 128), jnp.int32)
        for k in range(per):
            tile = jnp.where(lane // pad == k, ids[j * per + k], tile)
        tiles.append(jnp.broadcast_to(tile, (pad, 128)))
    sub = lax.broadcasted_iota(jnp.int32, (pad, 128), 0)
    slot, inner = sub // rows, sub % rows

    def mark(o, carry):
        band, col_band = o // nc, lax.rem(o, nc)
        grid_row = rb[band] + slot // CMAX
        grid_col = cb[col_band] + slot % CMAX
        inside = (grid_row < rb[band + 1]) & (grid_col < cb[col_band + 1]) & (slot < own)
        wanted = jnp.where(inside, (grid_row * grid_cols + grid_col) * rows + inner, -2)
        for j, tile in enumerate(tiles):
            onehot[pl.ds(pl.multiple_of(o * pad, pad), pad), j * 128:(j + 1) * 128] = (
                wanted == tile
            ).astype(jnp.float32)
        return carry

    lax.fori_loop(0, n, mark, 0)

    pltpu.make_async_copy(
        recv1.at[pl.ds(0, (n - 1) * pad)], recv1.at[pl.ds(0, (n - 1) * pad)], many_sem.at[3]
    ).wait()
    got = recv1[...]
    high = got.astype(jnp.bfloat16)
    rest = got - high.astype(jnp.float32)
    middle = rest.astype(jnp.bfloat16)
    low = (rest - middle.astype(jnp.float32)).astype(jnp.bfloat16)
    table = onehot[...].astype(jnp.bfloat16)
    dot = functools.partial(jnp.dot, preferred_element_type=jnp.float32)
    send2[...] = dot(table, high) + (dot(table, middle) + dot(table, low))
    recv2[pl.ds(pl.multiple_of(me * pad, pad), pad), :] = send2[pl.ds(pl.multiple_of(me * pad, pad), pad), :]

    def send_sums(to, where):
        pltpu.make_async_remote_copy(
            src_ref=send2.at[pl.ds(pl.multiple_of(to * pad, pad), pad)],
            dst_ref=recv2.at[pl.ds(pl.multiple_of(me * pad, pad), pad)],
            send_sem=many_sem.at[4], recv_sem=many_sem.at[5],
            device_id=where, device_id_type=MESH,
        ).start()

    others(send_sums)
    counts = jnp.sum(onehot[pl.ds(pl.multiple_of(me * pad, pad), pad), :], axis=1, keepdims=True)
    for load in loads[2:5]:
        load.wait()
    pltpu.make_async_copy(
        recv2.at[pl.ds(0, (n - 1) * pad)], recv2.at[pl.ds(0, (n - 1) * pad)], many_sem.at[5]
    ).wait()

    for s in range(own):
        for q in range(rows):
            sums_v[rows_of(q, n, rows), :] = recv2[rows_of(s * rows + q, n, pad), :]
        changed = jnp.broadcast_to(counts[s * rows:s * rows + 1, :], (side, side)) > 0.5
        averaged = sums_v[...] / n
        old = mas_v[s]
        first = BETA_ONE * mo1_v[s] + (1.0 - BETA_ONE) * averaged
        second = BETA_TWO * mo2_v[s] + (1.0 - BETA_TWO) * averaged * averaged
        direction = (
            first / CORRECT_ONE / (jnp.sqrt(second / CORRECT_TWO) + EPSILON) + DECAY_RATE * old
        )
        dir_v[s] = jnp.where(changed, direction, 0.0).astype(jnp.bfloat16)
        mas_v[s] = jnp.where(changed, old - LEARN_RATE * direction, old)
        mo1_v[s] = jnp.where(changed, first, mo1_v[s])
        mo2_v[s] = jnp.where(changed, second, mo2_v[s])

    def piece(dev_row, dev_col, half=None):
        start = (dev_row * nc + dev_col) * own
        if half is None:
            return around.at[pl.ds(start, own)]
        return around.at[pl.ds(start + half * (own // 2), own // 2)]

    def hop(ref, kind, index, where, src=None):
        pltpu.make_async_remote_copy(
            src_ref=ref if src is None else src, dst_ref=ref, send_sem=hop_send, recv_sem=hop_sem.at[kind, index],
            device_id=where, device_id_type=MESH,
        ).start()

    def landed(ref, kind, index):
        pltpu.make_async_copy(ref, ref, hop_sem.at[kind, index]).wait()

    own_piece = pltpu.make_async_copy(dir_v, piece(r, c), out_sem.at[4])
    own_piece.start()
    stores = [
        pltpu.make_async_copy(a, b, out_sem.at[1 + i])
        for i, (a, b) in enumerate(((mas_v, master_out), (mo1_v, moment1_out), (mo2_v, moment2_out)))
    ]
    if nr == 8 and own % 2 == 0:
        near = r + 1 - 2 * lax.rem(r, 2)
        beside = r + 2 - 4 * lax.rem(r // 2, 2)
        across = r + 4 - 8 * lax.rem(r // 4, 2)
        far = beside + 4 - 8 * lax.rem(beside // 4, 2)
        for k in range(1, nc):
            hop(piece(r, c), 0, c, (r, lax.rem(c + k, nc)), dir_v)

        def spread(z, src=None):
            hop(piece(r, z), 1, z, (beside, c), src)
            hop(piece(r, z), 2, z, (across, c), src)
            hop(piece(r, z), 5, z, (near, c), src)

        def relay(z):
            landed(piece(beside, z), 1, z)
            hop(piece(beside, z, 0), 3, z, (across, c))
            hop(piece(beside, z), 6, z, (near, c))
            landed(piece(across, z), 2, z)
            hop(piece(across, z, 1), 4, z, (beside, c))
            hop(piece(across, z), 7, z, (near, c))

        def finish(z):
            landed(piece(far, z, 0), 3, z)
            landed(piece(far, z, 1), 4, z)
            hop(piece(far, z), 8, z, (near, c))

        for k in range(nc + 2):
            if k < nc:
                z = lax.rem(c + k, nc)
                if k:
                    landed(piece(r, z), 0, z)
                spread(z, None if k else dir_v)
                if k == 0:
                    for store in stores:
                        store.start()
            if 1 <= k < nc + 1:
                relay(lax.rem(c + k - 1, nc))
            if k >= 2:
                finish(lax.rem(c + k - 2, nc))
        nears = (near, near + 2 - 4 * lax.rem(near // 2, 2))
        nears = nears + tuple(v + 4 - 8 * lax.rem(v // 4, 2) for v in nears)
        for k in range(nc):
            z = lax.rem(c + k, nc)
            landed(piece(nears[0], z), 5, z)
            landed(piece(nears[1], z), 6, z)
            landed(piece(nears[2], z), 7, z)
            landed(piece(nears[3], z), 8, z)
    else:
        others(lambda to, where: hop(piece(r, c), 0, 0, where, dir_v))
        for store in stores:
            store.start()
        landed(around.at[pl.ds(0, (n - 1) * own)], 0, 0)

    for i, ref in ((0, ids.at[pl.ds(0, n - 1)]), (2, send1.at[pl.ds(0, (n - 1) * pad)]), (4, send2.at[pl.ds(0, (n - 1) * pad)])):
        pltpu.make_async_copy(ref, ref, many_sem.at[i]).wait()
    landed_all = around.at[pl.ds(0, (n - 1) * own)]
    pltpu.make_async_copy(landed_all, landed_all, hop_send).wait()
    keep.wait()
    for store in stores:
        store.wait()
    own_piece.wait()


def place(
    nr, nc, rb, cb, error_in, master_in, moment1_in, moment2_in, around,
    error_out, master_out, moment1_out, moment2_out, step_out,
    err_v, mas_v, mo1_v, mo2_v, step_v, in_sem, out_sem, step_sem,
):
    blocks, own = step_out.shape[0], master_in.shape[0]
    grid_cols = nc - nc // 4
    pieces = 4
    part = blocks // pieces
    trips = [
        (error_in.at[pl.ds(i * part, part)], err_v.at[pl.ds(i * part, part)], error_out.at[pl.ds(i * part, part)])
        for i in range(pieces)
    ]
    trips += [
        (master_in, mas_v, master_out), (moment1_in, mo1_v, moment1_out), (moment2_in, mo2_v, moment2_out)
    ]
    ins = [pltpu.make_async_copy(a, b, in_sem.at[i]) for i, (a, b, _) in enumerate(trips)]
    outs = [pltpu.make_async_copy(b, c, out_sem.at[i]) for i, (_, b, c) in enumerate(trips)]
    for copy in ins:
        copy.start()
    col_of = []
    for grid_col in range(grid_cols):
        band = jnp.int32(0)
        for i in range(1, nc):
            band += (cb[i] <= grid_col).astype(jnp.int32)
        col_of.append(band * own + grid_col - cb[band])
    for grid_row in range(blocks // grid_cols):
        band = jnp.int32(0)
        for i in range(1, nr):
            band += (rb[i] <= grid_row).astype(jnp.int32)
        base = band * nc * own + (grid_row - rb[band]) * CMAX
        for grid_col in range(grid_cols):
            b = grid_row * grid_cols + grid_col
            slot = jnp.clip(base + col_of[grid_col], 0, nr * nc * own - 1)
            pltpu.make_async_copy(around.at[slot], step_v.at[b], step_sem.at[0]).start()
    for copy, then in zip(ins, outs):
        copy.wait()
        then.start()
    pltpu.make_async_copy(around.at[pl.ds(0, blocks)], step_v, step_sem.at[0]).wait()
    steps = pltpu.make_async_copy(step_v, step_out, step_sem.at[1])
    steps.start()
    for copy in outs:
        copy.wait()
    steps.wait()


def solution(mesh):
    nr, nc = mesh.shape["row"], mesh.shape["col"]
    n = nr * nc

    def local(grad, error, sel_blocks, row_bounds, col_bounds, master, moment1, moment2):
        blocks, side, _ = grad.shape
        picks, own = sel_blocks.shape[1], master.shape[0]
        rows = side // n
        pad = -(-max(picks, own) * rows // 8) * 8
        f32, bf16 = jnp.float32, jnp.bfloat16
        smem = pl.BlockSpec(memory_space=pltpu.SMEM)
        anywhere = pl.BlockSpec(memory_space=pl.ANY)
        slots = jax.ShapeDtypeStruct(master.shape, f32)
        parts = pl.pallas_call(
            functools.partial(kernel, nr, nc, rows, pad),
            out_shape=(
                jax.ShapeDtypeStruct(error.shape, f32), slots, slots, slots,
                jax.ShapeDtypeStruct((n * own, side, side), bf16),
            ),
            in_specs=[pl.BlockSpec(memory_space=pltpu.HBM)] * 8,
            out_specs=[anywhere] * 5,
            scratch_shapes=[
                pltpu.SMEM(sel_blocks.shape, jnp.int32),
                pltpu.SMEM(row_bounds.shape, jnp.int32),
                pltpu.SMEM(col_bounds.shape, jnp.int32),
                pltpu.VMEM(grad.shape, bf16),
                pltpu.VMEM(error.shape, f32),
                pltpu.VMEM(master.shape, f32),
                pltpu.VMEM(master.shape, f32),
                pltpu.VMEM(master.shape, f32),
                pltpu.VMEM((side, side), f32),
                pltpu.VMEM((side, side), f32),
                pltpu.VMEM((1, 128), jnp.int32),
                pltpu.VMEM((n, 1, 128), jnp.int32),
                pltpu.VMEM((n * pad, side), f32),
                pltpu.VMEM((n * pad, side), f32),
                pltpu.VMEM((n * pad, n * pad), f32),
                pltpu.VMEM((n * pad, side), f32),
                pltpu.VMEM((n * pad, side), f32),
                pltpu.VMEM(master.shape, bf16),
                pltpu.SemaphoreType.DMA((8,)),
                pltpu.SemaphoreType.DMA((5,)),
                pltpu.SemaphoreType.DMA((6,)),
                pltpu.SemaphoreType.DMA((9, nc)),
                pltpu.SemaphoreType.DMA,
            ],
            compiler_params=pltpu.CompilerParams(
                collective_id=0, has_side_effects=True, vmem_limit_bytes=64 * 1024 * 1024
            ),
        )(sel_blocks, row_bounds, col_bounds, grad, error, master, moment1, moment2)
        return pl.pallas_call(
            functools.partial(place, nr, nc),
            out_shape=(
                jax.ShapeDtypeStruct(error.shape, f32), slots, slots, slots,
                jax.ShapeDtypeStruct(grad.shape, bf16),
            ),
            in_specs=[smem] * 2 + [anywhere] * 5,
            out_specs=[pl.BlockSpec(memory_space=pltpu.HBM)] * 5,
            scratch_shapes=[
                pltpu.VMEM(error.shape, f32),
                pltpu.VMEM(master.shape, f32),
                pltpu.VMEM(master.shape, f32),
                pltpu.VMEM(master.shape, f32),
                pltpu.VMEM(grad.shape, bf16),
                pltpu.SemaphoreType.DMA((7,)),
                pltpu.SemaphoreType.DMA((7,)),
                pltpu.SemaphoreType.DMA((2,)),
            ],
            compiler_params=pltpu.CompilerParams(vmem_limit_bytes=64 * 1024 * 1024),
        )(row_bounds, col_bounds, *parts)

    whole = P(("row", "col"), None, None)
    return jax.shard_map(
        local,
        mesh=mesh,
        in_specs=(whole, whole, P(("row", "col"), None), P(), P(), whole, whole, whole),
        out_specs=(whole, whole, whole, whole, P()),
        check_vma=False,
    )
```

```python
import functools

import jax
import jax.numpy as jnp
from jax import lax
from jax.experimental import pallas as pl
from jax.experimental.pallas import tpu as pltpu
from jax.sharding import PartitionSpec as P

CMAX = 1
BETA_ONE = 0.9
BETA_TWO = 0.95
EPSILON = 1e-08
DECAY_RATE = 0.1
LEARN_RATE = 0.01
CORRECT_ONE = 1.0 - 0.9**10
CORRECT_TWO = 1.0 - 0.95**10
MESH = pl.DeviceIdType.MESH


def rows_of(start, size, stride):
    return pl.ds(start, size) if stride == 1 else pl.ds(start, size, stride=stride)


def update(totals, master, moment1, moment2, n):
    averaged = totals / n
    first = BETA_ONE * moment1 + (1.0 - BETA_ONE) * averaged
    second = BETA_TWO * moment2 + (1.0 - BETA_TWO) * averaged * averaged
    direction = (
        first / CORRECT_ONE / (jnp.sqrt(second / CORRECT_TWO) + EPSILON) + DECAY_RATE * master
    )
    return (master - LEARN_RATE * direction, first, second, direction)


def band_of(bounds, bands, position):
    band = jnp.int32(0)
    for i in range(1, bands):
        band += (bounds[i] <= position).astype(jnp.int32)
    return band


def kernel(
    nr, nc, rows, pad,
    sel_hbm, rb_hbm, cb_hbm, grad, error, master, moment1, moment2,
    error_out, sums_out, counts_out, around,
    sel, rb, cb, grad_v, err_v, state, states, acc_v, id_mine, ids, send1, recv1,
    send2, recv2, sums_v, sums_g, slots_v, counts_v, dir_v,
    local_sem, out_sem, many_sem, hop_sem, hop_send,
):
    n = nr * nc
    blocks, side = grad.shape[0], grad.shape[1]
    picks, own = sel.shape[1], master.shape[0]
    grid_cols = nc - nc // 4
    grid_rows = blocks // grid_cols
    coarse = rows * nc
    band_rows = grid_rows * rows
    r, c = lax.axis_index("row"), lax.axis_index("col")
    me = r * nc + c

    def others(body):
        def step(k, carry):
            to = lax.rem(me + k, n)
            body(to, (to // nc, lax.rem(to, nc)))
            return carry
        lax.fori_loop(1, n, step, 0)

    def send(src, dst, kind, where):
        pltpu.make_async_remote_copy(
            src_ref=src, dst_ref=dst, send_sem=many_sem.at[kind], recv_sem=many_sem.at[kind + 1],
            device_id=where, device_id_type=MESH,
        ).start()

    def row_peers(body):
        for k in range(1, nr):
            body(lax.rem(r + k, nr))

    def col_peers(body):
        for k in range(1, nc):
            body(lax.rem(c + k, nc))

    def bytes_of(ref, index):
        pltpu.make_async_copy(ref, ref, many_sem.at[index]).wait()

    barrier = pltpu.get_barrier_semaphore()
    loads = [
        pltpu.make_async_copy(a, b, local_sem.at[i])
        for i, (a, b) in enumerate(
            (
                (sel_hbm, sel), (rb_hbm, rb), (cb_hbm, cb), (grad, grad_v), (error, err_v),
                (master, state.at[0]), (moment1, state.at[1]), (moment2, state.at[2]),
            )
        )
    ]
    for load in loads:
        load.start()
    others(lambda to, where: pl.semaphore_signal(barrier, inc=1, device_id=where, device_id_type=MESH))
    for load in loads[:3]:
        load.wait()

    lane = lax.broadcasted_iota(jnp.int32, (1, 128), 1)
    part = lane % pad
    mine = jnp.full((1, 128), -1, jnp.int32)
    for s in range(picks):
        mine = jnp.where(part // rows == s, sel[0, s] * rows + part % rows, mine)
    id_mine[...] = mine
    ids[pl.ds(me, 1)] = mine[None]

    loads[3].wait()
    loads[4].wait()
    if pad > picks * rows:
        send1[...] = jnp.zeros_like(send1)
    for s in range(picks):
        pick = jnp.clip(sel[0, s], 0, blocks - 1)
        acc_v[...] = grad_v[pick].astype(jnp.float32) + err_v[pick]
        for q in range(rows):
            send1[rows_of(s * rows + q, n, pad), :] = acc_v[rows_of(q, n, rows), :]
    here = pl.ds(pl.multiple_of(me * pad, pad), pad)
    recv1[here, :] = send1[here, :]

    pl.semaphore_wait(barrier, n - 1)
    col_peers(lambda z: send(id_mine, ids.at[me], 0, (r, z)))
    others(lambda to, where: send(
        send1.at[pl.ds(pl.multiple_of(to * pad, pad), pad)], recv1.at[here], 2, where))
    bytes_of(ids.at[pl.ds(0, nc - 1)], 1)
    line = ids.at[pl.ds(r * nc, nc)]
    row_peers(lambda y: send(line, line, 6, (y, c)))

    for load in loads[5:]:
        load.wait()
    row_peers(lambda y: send(
        state.at[:, :, pl.ds(pl.multiple_of(y * coarse, coarse), coarse), :], states.at[r], 8, (y, c)))
    states[r] = state[:, :, pl.ds(pl.multiple_of(r * coarse, coarse), coarse), :]

    def clear(b, carry):
        chosen = (sel[0, 0] == b).astype(jnp.float32)
        for s in range(1, picks):
            chosen += (sel[0, s] == b).astype(jnp.float32)
        err_v[b] = (grad_v[b].astype(jnp.float32) + err_v[b]) * (1.0 - chosen)
        return carry

    lax.fori_loop(0, blocks, clear, 0)
    keep = pltpu.make_async_copy(err_v, error_out, out_sem.at[0])
    keep.start()

    bytes_of(ids.at[pl.ds(0, (nr - 1) * nc)], 7)
    per = 128 // pad
    tiles = []
    for j in range(n * pad // 128):
        tile = jnp.zeros((1, 128), jnp.int32)
        for k in range(per):
            tile = jnp.where(lane // pad == k, ids[j * per + k], tile)
        tiles.append(tile)

    def table_of(wanted):
        return [(wanted == tile).astype(jnp.float32) for tile in tiles]

    def tally(wanted):
        return jnp.sum(functools.reduce(jnp.add, table_of(wanted)), axis=1, keepdims=True)

    index = lax.broadcasted_iota(jnp.int32, (band_rows, 128), 0)
    table = []
    for band in range(nc):
        column = jnp.full((band_rows, 128), cb[band], jnp.int32)
        wanted = (index // rows * grid_cols + column) * rows + index % rows
        wanted = jnp.where(column < cb[band + 1], wanted, -2)
        table.append(jnp.concatenate(table_of(wanted), axis=1))
    table = jnp.concatenate(table, axis=0).astype(jnp.bfloat16)

    index = lax.broadcasted_iota(jnp.int32, (grid_rows * coarse, 128), 0)
    column = jnp.full((grid_rows * coarse, 128), cb[c], jnp.int32)
    wanted = jnp.where(column < cb[c + 1], (index // coarse * grid_cols + column) * rows, -2)
    counts = tally(wanted)
    slot = lax.broadcasted_iota(jnp.int32, (8, 128), 0)
    column = jnp.full((8, 128), cb[c], jnp.int32)
    inside = (column < cb[c + 1]) & (slot < own) & (rb[r] + slot < rb[r + 1])
    wanted = jnp.where(inside, ((rb[r] + slot) * grid_cols + column) * rows, -2)
    counts_v[...] = jnp.broadcast_to(tally(wanted), (8, 128))
    count_store = pltpu.make_async_copy(counts_v, counts_out, out_sem.at[1])
    count_store.start()

    bytes_of(recv1.at[pl.ds(0, (n - 1) * pad)], 3)
    got = recv1[...]
    high = got.astype(jnp.bfloat16)
    rest = got - high.astype(jnp.float32)
    middle = rest.astype(jnp.bfloat16)
    low = (rest - middle.astype(jnp.float32)).astype(jnp.bfloat16)
    dot = functools.partial(jnp.dot, preferred_element_type=jnp.float32)
    send2[...] = dot(table, high) + (dot(table, middle) + dot(table, low))
    band_here = pl.ds(pl.multiple_of(c * band_rows, 8), band_rows)
    col_peers(lambda z: send(
        send2.at[pl.ds(pl.multiple_of(z * band_rows, 8), band_rows)], recv2.at[band_here], 4, (r, z)))
    recv2[band_here, :] = send2[band_here, :]
    bytes_of(states.at[pl.ds(0, nr - 1)], 9)
    bytes_of(recv2.at[pl.ds(0, (nc - 1) * band_rows)], 5)

    for z in range(nc):
        for q in range(rows):
            sums_v[rows_of(z * rows + q, grid_rows, coarse), :] = recv2[
                rows_of(z * band_rows + q, grid_rows, rows), :]
    for g in range(grid_rows):
        band = band_of(rb, nr, g)
        offset = jnp.clip(g - rb[band], 0, own - 1)
        span = slice(g * coarse, (g + 1) * coarse)
        changed = jnp.broadcast_to(counts[span, :], (coarse, side)) > 0.5
        sums_g[g] = sums_v[span, :]
        direction = update(
            sums_v[span, :], states[band, 0, offset], states[band, 1, offset], states[band, 2, offset], n
        )[3]
        dir_v[g] = jnp.where(changed, direction, 0.0).astype(jnp.bfloat16)

    half = grid_rows // 2

    def piece(dev_row, dev_col, part=None):
        if part is None:
            return around.at[dev_row * nc + dev_col]
        return around.at[dev_row * nc + dev_col, pl.ds(part * half, half)]

    def hop(ref, kind, index, where, src=None):
        pltpu.make_async_remote_copy(
            src_ref=ref if src is None else src, dst_ref=ref, send_sem=hop_send,
            recv_sem=hop_sem.at[kind, index], device_id=where, device_id_type=MESH,
        ).start()

    def landed(ref, kind, index):
        pltpu.make_async_copy(ref, ref, hop_sem.at[kind, index]).wait()

    own_piece = pltpu.make_async_copy(dir_v, piece(r, c), out_sem.at[2])
    own_sums = pltpu.make_async_copy(
        slots_v.at[r], sums_out.at[:, pl.ds(pl.multiple_of(r * coarse, coarse), coarse), :], out_sem.at[3]
    )

    def send_sums():
        own_piece.start()
        for y in range(nr):
            for s in range(own):
                g = jnp.clip(rb[y] + s, 0, grid_rows - 1)
                slots_v[y, s] = sums_g[g]
        row_peers(lambda y: send(
            slots_v.at[y], sums_out.at[:, pl.ds(pl.multiple_of(r * coarse, coarse), coarse), :], 10, (y, c)))
        own_sums.start()

    if nr == 8 and grid_rows % 2 == 0:
        near = r + 1 - 2 * lax.rem(r, 2)
        beside = r + 2 - 4 * lax.rem(r // 2, 2)
        across = r + 4 - 8 * lax.rem(r // 4, 2)
        far = beside + 4 - 8 * lax.rem(beside // 4, 2)
        for k in range(1, nc):
            hop(piece(r, c), 0, c, (r, lax.rem(c + k, nc)), dir_v)

        def spread(z, src=None):
            hop(piece(r, z), 1, z, (beside, c), src)
            hop(piece(r, z), 2, z, (across, c), src)
            hop(piece(r, z), 5, z, (near, c), src)

        def relay(z):
            landed(piece(beside, z), 1, z)
            hop(piece(beside, z, 0), 3, z, (across, c))
            hop(piece(beside, z), 6, z, (near, c))
            landed(piece(across, z), 2, z)
            hop(piece(across, z, 1), 4, z, (beside, c))
            hop(piece(across, z), 7, z, (near, c))

        def finish(z):
            landed(piece(far, z, 0), 3, z)
            landed(piece(far, z, 1), 4, z)
            hop(piece(far, z), 8, z, (near, c))

        for k in range(nc + 2):
            if k < nc:
                z = lax.rem(c + k, nc)
                if k:
                    landed(piece(r, z), 0, z)
                spread(z, None if k else dir_v)
                if k == 0:
                    send_sums()
            if 1 <= k < nc + 1:
                relay(lax.rem(c + k - 1, nc))
            if k >= 2:
                finish(lax.rem(c + k - 2, nc))
        nears = (near, near + 2 - 4 * lax.rem(near // 2, 2))
        nears = nears + tuple(v + 4 - 8 * lax.rem(v // 4, 2) for v in nears)
        for k in range(nc):
            z = lax.rem(c + k, nc)
            for kind, dev_row in enumerate(nears):
                landed(piece(dev_row, z), 5 + kind, z)
    else:
        others(lambda to, where: hop(piece(r, c), 0, 0, where, dir_v))
        send_sums()
        landed(around.at[pl.ds(0, n - 1)], 0, 0)

    bytes_of(slots_v.at[pl.ds(0, nr - 1)], 11)
    for i, ref in (
        (0, ids.at[pl.ds(0, nc - 1)]), (2, send1.at[pl.ds(0, (n - 1) * pad)]),
        (4, send2.at[pl.ds(0, (nc - 1) * band_rows)]), (6, ids.at[pl.ds(0, (nr - 1) * nc)]),
        (8, states.at[pl.ds(0, nr - 1)]), (10, slots_v.at[pl.ds(0, nr - 1)]),
    ):
        bytes_of(ref, i)
    sent = around.at[pl.ds(0, n - 1)]
    pltpu.make_async_copy(sent, sent, hop_send).wait()
    for copy in (keep, count_store, own_piece, own_sums):
        copy.wait()


def place(
    nr, nc, cb, error_in, sums, counts, around, master, moment1, moment2,
    error_out, master_out, moment1_out, moment2_out, step_out,
    err_v, state, sums_v, counts_v, step_v, in_sem, out_sem, step_sem,
):
    blocks, own, side = error_in.shape[0], master.shape[0], master.shape[1]
    grid_cols = nc - nc // 4
    coarse = side // nr
    pieces = 4
    part = blocks // pieces
    cuts = [pl.ds(i * part, part) for i in range(pieces)]
    ins = [pltpu.make_async_copy(error_in.at[cut], err_v.at[cut], in_sem.at[i]) for i, cut in enumerate(cuts)]
    outs = [pltpu.make_async_copy(err_v.at[cut], error_out.at[cut], out_sem.at[i]) for i, cut in enumerate(cuts)]
    small = [
        pltpu.make_async_copy(a, b, in_sem.at[pieces + i])
        for i, (a, b) in enumerate((
            (master, state.at[0]), (moment1, state.at[1]), (moment2, state.at[2]),
            (sums, sums_v), (counts, counts_v),
        ))
    ]
    back = [
        pltpu.make_async_copy(state.at[i], b, out_sem.at[pieces + i])
        for i, b in enumerate((master_out, moment1_out, moment2_out))
    ]
    for copy in ins + small:
        copy.start()
    for col in range(grid_cols):
        band = band_of(cb, nc, col)
        for y in range(nr):
            pltpu.make_async_copy(
                around.at[y * nc + band], step_v.at[:, col, pl.ds(y * coarse, coarse), :], step_sem.at[0]
            ).start()
    for copy, then in zip(ins, outs):
        copy.wait()
        then.start()
    for copy in small:
        copy.wait()
    for s in range(own):
        changed = jnp.broadcast_to(counts_v[s:s + 1, :], (side, 128)) > 0.5
        old = [state[i, s] for i in range(3)]
        fresh = update(sums_v[s], *old, nr * nc)
        for i in range(3):
            state[i, s] = jnp.where(changed, fresh[i], old[i])
    for copy in back:
        copy.start()
    pltpu.make_async_copy(step_v, step_v, step_sem.at[0]).wait()
    steps = pltpu.make_async_copy(step_v, step_out, step_sem.at[1])
    steps.start()
    for copy in outs + back + [steps]:
        copy.wait()


def solution(mesh):
    nr, nc = mesh.shape["row"], mesh.shape["col"]
    n = nr * nc

    def local(grad, error, sel_blocks, row_bounds, col_bounds, master, moment1, moment2):
        blocks, side, _ = grad.shape
        picks, own = sel_blocks.shape[1], master.shape[0]
        rows, coarse = side // n, side // nr
        grid_cols = nc - nc // 4
        grid_rows = blocks // grid_cols
        pad = -(-picks * rows // 8) * 8
        f32, bf16, i32 = jnp.float32, jnp.bfloat16, jnp.int32
        anywhere = pl.BlockSpec(memory_space=pl.ANY)
        slots = jax.ShapeDtypeStruct(master.shape, f32)
        dma = pltpu.SemaphoreType.DMA
        new_error, sums, counts, around = pl.pallas_call(
            functools.partial(kernel, nr, nc, rows, pad),
            out_shape=(
                jax.ShapeDtypeStruct(error.shape, f32), slots,
                jax.ShapeDtypeStruct((8, 128), f32),
                jax.ShapeDtypeStruct((n, grid_rows, coarse, side), bf16),
            ),
            in_specs=[anywhere] * 8,
            out_specs=[anywhere] * 4,
            scratch_shapes=[
                pltpu.SMEM(sel_blocks.shape, i32),
                pltpu.SMEM(row_bounds.shape, i32),
                pltpu.SMEM(col_bounds.shape, i32),
                pltpu.VMEM(grad.shape, bf16),
                pltpu.VMEM(error.shape, f32),
                pltpu.VMEM((3,) + master.shape, f32),
                pltpu.VMEM((nr, 3, own, coarse, side), f32),
                pltpu.VMEM((side, side), f32),
                pltpu.VMEM((1, 128), i32),
                pltpu.VMEM((n, 1, 128), i32),
                pltpu.VMEM((n * pad, side), f32),
                pltpu.VMEM((n * pad, side), f32),
                pltpu.VMEM((nc * grid_rows * rows, side), f32),
                pltpu.VMEM((nc * grid_rows * rows, side), f32),
                pltpu.VMEM((grid_rows * coarse, side), f32),
                pltpu.VMEM((grid_rows, coarse, side), f32),
                pltpu.VMEM((nr, own, coarse, side), f32),
                pltpu.VMEM((8, 128), f32),
                pltpu.VMEM((grid_rows, coarse, side), bf16),
                dma((8,)), dma((4,)), dma((12,)), dma((9, nc)), dma,
            ],
            compiler_params=pltpu.CompilerParams(
                collective_id=0, has_side_effects=True, vmem_limit_bytes=64 * 1024 * 1024
            ),
        )(sel_blocks, row_bounds, col_bounds, grad, error, master, moment1, moment2)
        outs = pl.pallas_call(
            functools.partial(place, nr, nc),
            out_shape=(
                jax.ShapeDtypeStruct(error.shape, f32), slots, slots, slots,
                jax.ShapeDtypeStruct((grid_rows, grid_cols, side, side), bf16),
            ),
            in_specs=[pl.BlockSpec(memory_space=pltpu.SMEM)] + [anywhere] * 7,
            out_specs=[anywhere] * 5,
            scratch_shapes=[
                pltpu.VMEM(error.shape, f32),
                pltpu.VMEM((3,) + master.shape, f32),
                pltpu.VMEM(master.shape, f32),
                pltpu.VMEM((8, 128), f32),
                pltpu.VMEM((grid_rows, grid_cols, side, side), bf16),
                dma((9,)), dma((7,)), dma((2,)),
            ],
            compiler_params=pltpu.CompilerParams(vmem_limit_bytes=64 * 1024 * 1024),
        )(col_bounds, new_error, sums, counts, around, master, moment1, moment2)
        return outs[:4] + (outs[4].reshape(grad.shape),)

    whole = P(("row", "col"), None, None)
    return jax.shard_map(
        local,
        mesh=mesh,
        in_specs=(whole, whole, P(("row", "col"), None), P(), P(), whole, whole, whole),
        out_specs=(whole, whole, whole, whole, P()),
        check_vma=False,
    )
```

```python
import functools

import jax
import jax.numpy as jnp
from jax import lax
from jax.experimental import pallas as pl
from jax.experimental.pallas import tpu as pltpu
from jax.sharding import PartitionSpec as P

CMAX = 1
BETA_ONE = 0.9
BETA_TWO = 0.95
EPSILON = 1e-08
DECAY_RATE = 0.1
LEARN_RATE = 0.01
CORRECT_ONE = 1.0 - 0.9**10
CORRECT_TWO = 1.0 - 0.95**10
MESH = pl.DeviceIdType.MESH


def rows_of(start, size, stride):
    return pl.ds(start, size) if stride == 1 else pl.ds(start, size, stride=stride)


def update(totals, master, moment1, moment2, n):
    averaged = totals / n
    first = BETA_ONE * moment1 + (1.0 - BETA_ONE) * averaged
    second = BETA_TWO * moment2 + (1.0 - BETA_TWO) * averaged * averaged
    direction = (
        first / CORRECT_ONE / (jnp.sqrt(second / CORRECT_TWO) + EPSILON) + DECAY_RATE * master
    )
    return (master - LEARN_RATE * direction, first, second, direction)


def band_of(bounds, bands, position):
    band = jnp.int32(0)
    for i in range(1, bands):
        band += (bounds[i] <= position).astype(jnp.int32)
    return band


def kernel(
    nr, nc, rows, pad,
    sel_hbm, rb_hbm, cb_hbm, grad, error, master, moment1, moment2,
    error_out, sums_out, counts_out, around,
    sel, rb, cb, grad_v, err_v, state, states, acc_v, id_mine, ids, send1, recv1,
    send2, recv2, sums_v, sums_g, slots_v, counts_v, dir_v, around_v,
    local_sem, out_sem, many_sem, hop_sem, hop_send,
):
    n = nr * nc
    blocks, side = grad.shape[0], grad.shape[1]
    picks, own = sel.shape[1], master.shape[0]
    grid_cols = nc - nc // 4
    grid_rows = blocks // grid_cols
    coarse = rows * nc
    band_rows = grid_rows * rows
    r, c = lax.axis_index("row"), lax.axis_index("col")
    me = r * nc + c

    def others(body):
        def step(k, carry):
            to = lax.rem(me + k, n)
            body(to, (lax.div(to, nc), lax.rem(to, nc)))
            return carry
        lax.fori_loop(1, n, step, 0, unroll=n <= 32)

    def send(src, dst, kind, where):
        pltpu.make_async_remote_copy(
            src_ref=src, dst_ref=dst, send_sem=many_sem.at[kind], recv_sem=many_sem.at[kind + 1],
            device_id=where, device_id_type=MESH,
        ).start()

    def row_peers(body):
        for k in range(1, nr):
            body(lax.rem(r + k, nr))

    def col_peers(body):
        for k in range(1, nc):
            body(lax.rem(c + k, nc))

    def bytes_of(ref, index):
        pltpu.make_async_copy(ref, ref, many_sem.at[index]).wait()

    barrier = pltpu.get_barrier_semaphore()
    loads = [
        pltpu.make_async_copy(a, b, local_sem.at[i])
        for i, (a, b) in enumerate(
            (
                (sel_hbm, sel), (rb_hbm, rb), (cb_hbm, cb), (grad, grad_v), (error, err_v),
                (master, state.at[0]), (moment1, state.at[1]), (moment2, state.at[2]),
            )
        )
    ]
    for load in loads:
        load.start()
    others(lambda to, where: pl.semaphore_signal(barrier, inc=1, device_id=where, device_id_type=MESH))
    for load in loads[:3]:
        load.wait()

    lane = lax.broadcasted_iota(jnp.int32, (1, 128), 1)
    part = lane % pad
    mine = jnp.full((1, 128), -1, jnp.int32)
    for s in range(picks):
        mine = jnp.where(part // rows == s, sel[0, s] * rows + part % rows, mine)
    id_mine[...] = mine
    ids[pl.ds(me, 1)] = mine[None]

    loads[3].wait()
    loads[4].wait()
    if pad > picks * rows:
        send1[...] = jnp.zeros_like(send1)
    for s in range(picks):
        pick = jnp.clip(sel[0, s], 0, blocks - 1)
        acc_v[...] = grad_v[pick].astype(jnp.float32) + err_v[pick]
        for q in range(rows):
            send1[rows_of(s * rows + q, n, pad), :] = acc_v[rows_of(q, n, rows), :]
    here = pl.ds(pl.multiple_of(me * pad, pad), pad)
    recv1[here, :] = send1[here, :]

    pl.semaphore_wait(barrier, n - 1)
    col_peers(lambda z: send(id_mine, ids.at[me], 0, (r, z)))
    others(lambda to, where: send(
        send1.at[pl.ds(pl.multiple_of(to * pad, pad), pad)], recv1.at[here], 2, where))
    bytes_of(ids.at[pl.ds(0, nc - 1)], 1)
    line = ids.at[pl.ds(r * nc, nc)]
    row_peers(lambda y: send(line, line, 6, (y, c)))

    for load in loads[5:]:
        load.wait()
    row_peers(lambda y: send(
        state.at[:, :, pl.ds(pl.multiple_of(y * coarse, coarse), coarse), :], states.at[r], 8, (y, c)))
    states[r] = state[:, :, pl.ds(pl.multiple_of(r * coarse, coarse), coarse), :]

    def clear(b, carry):
        chosen = (sel[0, 0] == b).astype(jnp.float32)
        for s in range(1, picks):
            chosen += (sel[0, s] == b).astype(jnp.float32)
        err_v[b] = (grad_v[b].astype(jnp.float32) + err_v[b]) * (1.0 - chosen)
        return carry

    lax.fori_loop(0, blocks, clear, 0)
    keep = pltpu.make_async_copy(err_v, error_out, out_sem.at[0])
    keep.start()

    bytes_of(ids.at[pl.ds(0, (nr - 1) * nc)], 7)
    per = 128 // pad
    tiles = []
    for j in range(n * pad // 128):
        tile = jnp.zeros((1, 128), jnp.int32)
        for k in range(per):
            tile = jnp.where(lane // pad == k, ids[j * per + k], tile)
        tiles.append(tile)

    def table_of(wanted):
        return [(wanted == tile).astype(jnp.float32) for tile in tiles]

    def tally(wanted):
        return jnp.sum(functools.reduce(jnp.add, table_of(wanted)), axis=1, keepdims=True)

    index = lax.broadcasted_iota(jnp.int32, (band_rows, 128), 0)
    table = []
    for band in range(nc):
        column = jnp.full((band_rows, 128), cb[band], jnp.int32)
        wanted = (index // rows * grid_cols + column) * rows + index % rows
        wanted = jnp.where(column < cb[band + 1], wanted, -2)
        table.append(jnp.concatenate(table_of(wanted), axis=1))
    table = jnp.concatenate(table, axis=0).astype(jnp.bfloat16)

    bytes_of(recv1.at[pl.ds(0, (n - 1) * pad)], 3)
    got = recv1[...]
    high = got.astype(jnp.bfloat16)
    rest = got - high.astype(jnp.float32)
    middle = rest.astype(jnp.bfloat16)
    low = (rest - middle.astype(jnp.float32)).astype(jnp.bfloat16)
    dot = functools.partial(jnp.dot, preferred_element_type=jnp.float32)
    send2[...] = dot(table, high) + (dot(table, middle) + dot(table, low))
    band_here = pl.ds(pl.multiple_of(c * band_rows, 8), band_rows)
    col_peers(lambda z: send(
        send2.at[pl.ds(pl.multiple_of(z * band_rows, 8), band_rows)], recv2.at[band_here], 4, (r, z)))
    recv2[band_here, :] = send2[band_here, :]

    index = lax.broadcasted_iota(jnp.int32, (grid_rows * coarse, 128), 0)
    column = jnp.full((grid_rows * coarse, 128), cb[c], jnp.int32)
    wanted = jnp.where(column < cb[c + 1], (index // coarse * grid_cols + column) * rows, -2)
    counts = tally(wanted)
    slot = lax.broadcasted_iota(jnp.int32, (8, 128), 0)
    column = jnp.full((8, 128), cb[c], jnp.int32)
    inside = (column < cb[c + 1]) & (slot < own) & (rb[r] + slot < rb[r + 1])
    wanted = jnp.where(inside, ((rb[r] + slot) * grid_cols + column) * rows, -2)
    counts_v[...] = jnp.broadcast_to(tally(wanted), (8, 128))
    count_store = pltpu.make_async_copy(counts_v, counts_out, out_sem.at[1])
    count_store.start()

    bytes_of(states.at[pl.ds(0, nr - 1)], 9)
    bytes_of(recv2.at[pl.ds(0, (nc - 1) * band_rows)], 5)

    for z in range(nc):
        for q in range(rows):
            sums_v[rows_of(z * rows + q, grid_rows, coarse), :] = recv2[
                rows_of(z * band_rows + q, grid_rows, rows), :]
    for g in range(grid_rows):
        band = band_of(rb, nr, g)
        offset = jnp.clip(g - rb[band], 0, own - 1)
        span = slice(g * coarse, (g + 1) * coarse)
        changed = jnp.broadcast_to(counts[span, :], (coarse, side)) > 0.5
        sums_g[g] = sums_v[span, :]
        direction = update(
            sums_v[span, :], states[band, 0, offset], states[band, 1, offset], states[band, 2, offset], n
        )[3]
        dir_v[g] = jnp.where(changed, direction, 0.0).astype(jnp.bfloat16)

    half = grid_rows // 2

    def piece(dev_row, dev_col, part=None):
        if part is None:
            return around_v.at[dev_row * nc + dev_col]
        return around_v.at[dev_row * nc + dev_col, pl.ds(part * half, half)]

    def stash(dev_row, dev_col, src=None):
        pltpu.make_async_copy(
            piece(dev_row, dev_col) if src is None else src, around.at[dev_row * nc + dev_col], out_sem.at[2]
        ).start()

    def hop(ref, kind, index, where, src=None):
        pltpu.make_async_remote_copy(
            src_ref=ref if src is None else src, dst_ref=ref, send_sem=hop_send,
            recv_sem=hop_sem.at[kind, index], device_id=where, device_id_type=MESH,
        ).start()

    def landed(ref, kind, index):
        pltpu.make_async_copy(ref, ref, hop_sem.at[kind, index]).wait()

    own_sums = pltpu.make_async_copy(
        slots_v.at[r], sums_out.at[:, pl.ds(pl.multiple_of(r * coarse, coarse), coarse), :], out_sem.at[3]
    )

    def send_sums():
        stash(r, c, dir_v)
        for y in range(nr):
            for s in range(own):
                g = jnp.clip(rb[y] + s, 0, grid_rows - 1)
                slots_v[y, s] = sums_g[g]
        row_peers(lambda y: send(
            slots_v.at[y], sums_out.at[:, pl.ds(pl.multiple_of(r * coarse, coarse), coarse), :], 10, (y, c)))
        own_sums.start()

    if nr == 8 and grid_rows % 2 == 0:
        near = r + 1 - 2 * lax.rem(r, 2)
        beside = r + 2 - 4 * lax.rem(r // 2, 2)
        across = r + 4 - 8 * lax.rem(r // 4, 2)
        far = beside + 4 - 8 * lax.rem(beside // 4, 2)
        order = [lax.rem(c + k, nc) for k in range(nc)]
        if nc == 4:
            upper = lax.div(c, 2)
            inner = c + upper * (3 - 2 * c)
            order = [c] + [z + upper * (3 - 2 * z) for z in (1 - inner, 2, 3)]
        for z in order[1:]:
            hop(piece(r, c), 0, c, (r, z), dir_v)

        def spread(z, src=None):
            hop(piece(r, z), 1, z, (beside, c), src)
            hop(piece(r, z), 2, z, (across, c), src)
            hop(piece(r, z), 5, z, (near, c), src)

        def relay(z):
            landed(piece(beside, z), 1, z)
            hop(piece(beside, z, 0), 3, z, (across, c))
            hop(piece(beside, z), 6, z, (near, c))
            landed(piece(across, z), 2, z)
            hop(piece(across, z, 1), 4, z, (beside, c))
            hop(piece(across, z), 7, z, (near, c))
            stash(beside, z)
            stash(across, z)

        def finish(z):
            landed(piece(far, z, 0), 3, z)
            landed(piece(far, z, 1), 4, z)
            hop(piece(far, z), 8, z, (near, c))
            stash(far, z)

        for k in range(nc + 2):
            if k < nc:
                z = order[k]
                if k:
                    landed(piece(r, z), 0, z)
                spread(z, None if k else dir_v)
                if k == 0:
                    send_sums()
                else:
                    stash(r, z)
            if 1 <= k < nc + 1:
                relay(order[k - 1])
            if k >= 2:
                finish(order[k - 2])
        nears = (near, near + 2 - 4 * lax.rem(near // 2, 2))
        nears = nears + tuple(v + 4 - 8 * lax.rem(v // 4, 2) for v in nears)
        for z in order:
            for kind, dev_row in enumerate(nears):
                landed(piece(dev_row, z), 5 + kind, z)
                stash(dev_row, z)
    else:
        others(lambda to, where: hop(piece(r, c), 0, 0, where, dir_v))
        send_sums()
        landed(around_v.at[pl.ds(0, n - 1)], 0, 0)
        others(lambda to, where: stash(*where))

    bytes_of(slots_v.at[pl.ds(0, nr - 1)], 11)
    for i, ref in (
        (0, ids.at[pl.ds(0, nc - 1)]), (2, send1.at[pl.ds(0, (n - 1) * pad)]),
        (4, send2.at[pl.ds(0, (nc - 1) * band_rows)]), (6, ids.at[pl.ds(0, (nr - 1) * nc)]),
        (8, states.at[pl.ds(0, nr - 1)]), (10, slots_v.at[pl.ds(0, nr - 1)]),
    ):
        bytes_of(ref, i)
    sent = around_v.at[pl.ds(0, n - 1)]
    pltpu.make_async_copy(sent, sent, hop_send).wait()
    stashed = pltpu.make_async_copy(around_v, around, out_sem.at[2])
    for copy in (keep, count_store, own_sums, stashed):
        copy.wait()


def place(
    nr, nc, cb, error_in, sums, counts, around, master, moment1, moment2,
    error_out, master_out, moment1_out, moment2_out, step_out,
    err_v, state, sums_v, counts_v, step_v, in_sem, out_sem, step_sem,
):
    blocks, own, side = error_in.shape[0], master.shape[0], master.shape[1]
    grid_cols = nc - nc // 4
    coarse = side // nr
    pieces = 4
    part = blocks // pieces
    cuts = [pl.ds(i * part, part) for i in range(pieces)]
    ins = [pltpu.make_async_copy(error_in.at[cut], err_v.at[cut], in_sem.at[i]) for i, cut in enumerate(cuts)]
    outs = [pltpu.make_async_copy(err_v.at[cut], error_out.at[cut], out_sem.at[i]) for i, cut in enumerate(cuts)]
    small = [
        pltpu.make_async_copy(a, b, in_sem.at[pieces + i])
        for i, (a, b) in enumerate((
            (master, state.at[0]), (moment1, state.at[1]), (moment2, state.at[2]),
            (sums, sums_v), (counts, counts_v),
        ))
    ]
    back = [
        pltpu.make_async_copy(state.at[i], b, out_sem.at[pieces + i])
        for i, b in enumerate((master_out, moment1_out, moment2_out))
    ]
    for copy in ins + small:
        copy.start()
    for col in range(grid_cols):
        band = band_of(cb, nc, col)
        for y in range(nr):
            pltpu.make_async_copy(
                around.at[y * nc + band], step_v.at[:, col, pl.ds(y * coarse, coarse), :], step_sem.at[0]
            ).start()
    for copy, then in zip(ins, outs):
        copy.wait()
        then.start()
    for copy in small:
        copy.wait()
    for s in range(own):
        changed = jnp.broadcast_to(counts_v[s:s + 1, :], (side, 128)) > 0.5
        old = [state[i, s] for i in range(3)]
        fresh = update(sums_v[s], *old, nr * nc)
        for i in range(3):
            state[i, s] = jnp.where(changed, fresh[i], old[i])
    for copy in back:
        copy.start()
    pltpu.make_async_copy(step_v, step_v, step_sem.at[0]).wait()
    steps = pltpu.make_async_copy(step_v, step_out, step_sem.at[1])
    steps.start()
    for copy in outs + back + [steps]:
        copy.wait()


def solution(mesh):
    nr, nc = mesh.shape["row"], mesh.shape["col"]
    n = nr * nc

    def local(grad, error, sel_blocks, row_bounds, col_bounds, master, moment1, moment2):
        blocks, side, _ = grad.shape
        picks, own = sel_blocks.shape[1], master.shape[0]
        rows, coarse = side // n, side // nr
        grid_cols = nc - nc // 4
        grid_rows = blocks // grid_cols
        pad = -(-picks * rows // 8) * 8
        f32, bf16, i32 = jnp.float32, jnp.bfloat16, jnp.int32
        anywhere = pl.BlockSpec(memory_space=pl.ANY)
        slots = jax.ShapeDtypeStruct(master.shape, f32)
        dma = pltpu.SemaphoreType.DMA
        new_error, sums, counts, around = pl.pallas_call(
            functools.partial(kernel, nr, nc, rows, pad),
            out_shape=(
                jax.ShapeDtypeStruct(error.shape, f32), slots,
                jax.ShapeDtypeStruct((8, 128), f32),
                jax.ShapeDtypeStruct((n, grid_rows, coarse, side), bf16),
            ),
            in_specs=[anywhere] * 8,
            out_specs=[anywhere] * 4,
            scratch_shapes=[
                pltpu.SMEM(sel_blocks.shape, i32),
                pltpu.SMEM(row_bounds.shape, i32),
                pltpu.SMEM(col_bounds.shape, i32),
                pltpu.VMEM(grad.shape, bf16),
                pltpu.VMEM(error.shape, f32),
                pltpu.VMEM((3,) + master.shape, f32),
                pltpu.VMEM((nr, 3, own, coarse, side), f32),
                pltpu.VMEM((side, side), f32),
                pltpu.VMEM((1, 128), i32),
                pltpu.VMEM((n, 1, 128), i32),
                pltpu.VMEM((n * pad, side), f32),
                pltpu.VMEM((n * pad, side), f32),
                pltpu.VMEM((nc * grid_rows * rows, side), f32),
                pltpu.VMEM((nc * grid_rows * rows, side), f32),
                pltpu.VMEM((grid_rows * coarse, side), f32),
                pltpu.VMEM((grid_rows, coarse, side), f32),
                pltpu.VMEM((nr, own, coarse, side), f32),
                pltpu.VMEM((8, 128), f32),
                pltpu.VMEM((grid_rows, coarse, side), bf16),
                pltpu.VMEM((n, grid_rows, coarse, side), bf16),
                dma((8,)), dma((4,)), dma((12,)), dma((9, nc)), dma,
            ],
            compiler_params=pltpu.CompilerParams(
                collective_id=0, has_side_effects=True, vmem_limit_bytes=64 * 1024 * 1024
            ),
        )(sel_blocks, row_bounds, col_bounds, grad, error, master, moment1, moment2)
        outs = pl.pallas_call(
            functools.partial(place, nr, nc),
            out_shape=(
                jax.ShapeDtypeStruct(error.shape, f32), slots, slots, slots,
                jax.ShapeDtypeStruct((grid_rows, grid_cols, side, side), bf16),
            ),
            in_specs=[pl.BlockSpec(memory_space=pltpu.SMEM)] + [anywhere] * 7,
            out_specs=[anywhere] * 5,
            scratch_shapes=[
                pltpu.VMEM(error.shape, f32),
                pltpu.VMEM((3,) + master.shape, f32),
                pltpu.VMEM(master.shape, f32),
                pltpu.VMEM((8, 128), f32),
                pltpu.VMEM((grid_rows, grid_cols, side, side), bf16),
                dma((9,)), dma((7,)), dma((2,)),
            ],
            compiler_params=pltpu.CompilerParams(vmem_limit_bytes=64 * 1024 * 1024),
        )(col_bounds, new_error, sums, counts, around, master, moment1, moment2)
        return outs[:4] + (outs[4].reshape(grad.shape),)

    whole = P(("row", "col"), None, None)
    return jax.shard_map(
        local,
        mesh=mesh,
        in_specs=(whole, whole, P(("row", "col"), None), P(), P(), whole, whole, whole),
        out_specs=(whole, whole, whole, whole, P()),
        check_vma=False,
    )
```

```python
import functools

import jax
import jax.numpy as jnp
from jax import lax
from jax.experimental import pallas as pl
from jax.experimental.pallas import tpu as pltpu
from jax.sharding import PartitionSpec as P

CMAX = 1
BETA_ONE = 0.9
BETA_TWO = 0.95
EPSILON = 1e-08
DECAY_RATE = 0.1
LEARN_RATE = 0.01
CORRECT_ONE = 1.0 - 0.9**10
CORRECT_TWO = 1.0 - 0.95**10
MESH = pl.DeviceIdType.MESH


def rows_of(start, size, stride):
    return pl.ds(start, size) if stride == 1 else pl.ds(start, size, stride=stride)


def update(totals, master, moment1, moment2, n):
    averaged = totals / n
    first = BETA_ONE * moment1 + (1.0 - BETA_ONE) * averaged
    second = BETA_TWO * moment2 + (1.0 - BETA_TWO) * averaged * averaged
    direction = (
        first / CORRECT_ONE / (jnp.sqrt(second / CORRECT_TWO) + EPSILON) + DECAY_RATE * master
    )
    return (master - LEARN_RATE * direction, first, second, direction)


def band_of(bounds, bands, position):
    band = jnp.int32(0)
    for i in range(1, bands):
        band += (bounds[i] <= position).astype(jnp.int32)
    return band


def kernel(
    nr, nc, rows, pad,
    sel_hbm, rb_hbm, cb_hbm, grad, error, master, moment1, moment2,
    error_out, sums_out, counts_out, around,
    sel, rb, cb, grad_v, err_v, state, states, acc_v, id_mine, ids, send1, recv1,
    send2, recv2, sums_v, sums_g, slots_v, counts_v, dir_v, around_v,
    local_sem, out_sem, many_sem, hop_sem, hop_send,
):
    n = nr * nc
    blocks, side = grad.shape[0], grad.shape[1]
    picks, own = sel.shape[1], master.shape[0]
    grid_cols = nc - nc // 4
    grid_rows = blocks // grid_cols
    coarse = rows * nc
    band_rows = grid_rows * rows
    r, c = lax.axis_index("row"), lax.axis_index("col")
    me = r * nc + c

    def others(body):
        def step(k, carry):
            to = lax.rem(me + k, n)
            body(to, (lax.div(to, nc), lax.rem(to, nc)))
            return carry
        lax.fori_loop(1, n, step, 0, unroll=n <= 32)

    def send(src, dst, kind, where):
        pltpu.make_async_remote_copy(
            src_ref=src, dst_ref=dst, send_sem=many_sem.at[kind], recv_sem=many_sem.at[kind + 1],
            device_id=where, device_id_type=MESH,
        ).start()

    def row_peers(body):
        for k in range(1, nr):
            body(lax.rem(r + k, nr))

    def col_peers(body):
        for k in range(1, nc):
            body(lax.rem(c + k, nc))

    def bytes_of(ref, index):
        pltpu.make_async_copy(ref, ref, many_sem.at[index]).wait()

    barrier = pltpu.get_barrier_semaphore()
    loads = [
        pltpu.make_async_copy(a, b, local_sem.at[i])
        for i, (a, b) in enumerate(
            (
                (sel_hbm, sel), (rb_hbm, rb), (cb_hbm, cb), (grad, grad_v), (error, err_v),
                (master, state.at[0]), (moment1, state.at[1]), (moment2, state.at[2]),
            )
        )
    ]
    for load in loads:
        load.start()
    others(lambda to, where: pl.semaphore_signal(barrier, inc=1, device_id=where, device_id_type=MESH))
    for load in loads[:3]:
        load.wait()

    lane = lax.broadcasted_iota(jnp.int32, (1, 128), 1)
    part = lane % pad
    mine = jnp.full((1, 128), -1, jnp.int32)
    for s in range(picks):
        mine = jnp.where(part // rows == s, sel[0, s] * rows + part % rows, mine)
    id_mine[...] = mine
    ids[pl.ds(me, 1)] = mine[None]

    loads[3].wait()
    loads[4].wait()
    if pad > picks * rows:
        send1[...] = jnp.zeros_like(send1)
    for s in range(picks):
        pick = jnp.clip(sel[0, s], 0, blocks - 1)
        acc_v[...] = grad_v[pick].astype(jnp.float32) + err_v[pick]
        for q in range(rows):
            send1[rows_of(s * rows + q, n, pad), :] = acc_v[rows_of(q, n, rows), :]
    here = pl.ds(pl.multiple_of(me * pad, pad), pad)
    recv1[here, :] = send1[here, :]

    pl.semaphore_wait(barrier, n - 1)
    col_peers(lambda z: send(id_mine, ids.at[me], 0, (r, z)))
    others(lambda to, where: send(
        send1.at[pl.ds(pl.multiple_of(to * pad, pad), pad)], recv1.at[here], 2, where))
    bytes_of(ids.at[pl.ds(0, nc - 1)], 1)
    line = ids.at[pl.ds(r * nc, nc)]
    row_peers(lambda y: send(line, line, 6, (y, c)))

    for load in loads[5:]:
        load.wait()
    row_peers(lambda y: send(
        state.at[:, :, pl.ds(pl.multiple_of(y * coarse, coarse), coarse), :], states.at[r], 8, (y, c)))
    states[r] = state[:, :, pl.ds(pl.multiple_of(r * coarse, coarse), coarse), :]

    bytes_of(ids.at[pl.ds(0, (nr - 1) * nc)], 7)
    per = 128 // pad
    tiles = []
    for j in range(n * pad // 128):
        tile = jnp.zeros((1, 128), jnp.int32)
        for k in range(per):
            tile = jnp.where(lane // pad == k, ids[j * per + k], tile)
        tiles.append(tile)

    def table_of(wanted):
        return [(wanted == tile).astype(jnp.float32) for tile in tiles]

    def tally(wanted):
        return jnp.sum(functools.reduce(jnp.add, table_of(wanted)), axis=1, keepdims=True)

    index = lax.broadcasted_iota(jnp.int32, (band_rows, 128), 0)
    table = []
    for band in range(nc):
        column = jnp.full((band_rows, 128), cb[band], jnp.int32)
        wanted = (index // rows * grid_cols + column) * rows + index % rows
        wanted = jnp.where(column < cb[band + 1], wanted, -2)
        table.append(jnp.concatenate(table_of(wanted), axis=1))
    table = jnp.concatenate(table, axis=0).astype(jnp.bfloat16)

    bytes_of(recv1.at[pl.ds(0, (n - 1) * pad)], 3)
    got = recv1[...]
    high = got.astype(jnp.bfloat16)
    rest = got - high.astype(jnp.float32)
    middle = rest.astype(jnp.bfloat16)
    low = (rest - middle.astype(jnp.float32)).astype(jnp.bfloat16)
    dot = functools.partial(jnp.dot, preferred_element_type=jnp.float32)
    send2[...] = dot(table, high) + (dot(table, middle) + dot(table, low))
    band_here = pl.ds(pl.multiple_of(c * band_rows, 8), band_rows)
    col_peers(lambda z: send(
        send2.at[pl.ds(pl.multiple_of(z * band_rows, 8), band_rows)], recv2.at[band_here], 4, (r, z)))
    recv2[band_here, :] = send2[band_here, :]

    index = lax.broadcasted_iota(jnp.int32, (grid_rows * coarse, 128), 0)
    column = jnp.full((grid_rows * coarse, 128), cb[c], jnp.int32)
    wanted = jnp.where(column < cb[c + 1], (index // coarse * grid_cols + column) * rows, -2)
    counts = tally(wanted)
    slot = lax.broadcasted_iota(jnp.int32, (8, 128), 0)
    column = jnp.full((8, 128), cb[c], jnp.int32)
    inside = (column < cb[c + 1]) & (slot < own) & (rb[r] + slot < rb[r + 1])
    wanted = jnp.where(inside, ((rb[r] + slot) * grid_cols + column) * rows, -2)
    counts_v[...] = jnp.broadcast_to(tally(wanted), (8, 128))
    count_store = pltpu.make_async_copy(counts_v, counts_out, out_sem.at[1])
    count_store.start()

    def clear(b, carry):
        chosen = (sel[0, 0] == b).astype(jnp.float32)
        for s in range(1, picks):
            chosen += (sel[0, s] == b).astype(jnp.float32)
        err_v[b] = (grad_v[b].astype(jnp.float32) + err_v[b]) * (1.0 - chosen)
        return carry

    lax.fori_loop(0, blocks, clear, 0)
    keep = pltpu.make_async_copy(err_v, error_out, out_sem.at[0])
    keep.start()

    bytes_of(states.at[pl.ds(0, nr - 1)], 9)
    bytes_of(recv2.at[pl.ds(0, (nc - 1) * band_rows)], 5)

    for z in range(nc):
        for q in range(rows):
            sums_v[rows_of(z * rows + q, grid_rows, coarse), :] = recv2[
                rows_of(z * band_rows + q, grid_rows, rows), :]
    for g in range(grid_rows):
        band = band_of(rb, nr, g)
        offset = jnp.clip(g - rb[band], 0, own - 1)
        span = slice(g * coarse, (g + 1) * coarse)
        changed = jnp.broadcast_to(counts[span, :], (coarse, side)) > 0.5
        sums_g[g] = sums_v[span, :]
        direction = update(
            sums_v[span, :], states[band, 0, offset], states[band, 1, offset], states[band, 2, offset], n
        )[3]
        dir_v[g] = jnp.where(changed, direction, 0.0).astype(jnp.bfloat16)

    half = grid_rows // 2

    def piece(dev_row, dev_col, part=None):
        if part is None:
            return around_v.at[dev_row * nc + dev_col]
        return around_v.at[dev_row * nc + dev_col, pl.ds(part * half, half)]

    def stash(dev_row, dev_col, src=None):
        pltpu.make_async_copy(
            piece(dev_row, dev_col) if src is None else src, around.at[dev_row * nc + dev_col], out_sem.at[2]
        ).start()

    def hop(ref, kind, index, where, src=None):
        pltpu.make_async_remote_copy(
            src_ref=ref if src is None else src, dst_ref=ref, send_sem=hop_send,
            recv_sem=hop_sem.at[kind, index], device_id=where, device_id_type=MESH,
        ).start()

    def landed(ref, kind, index):
        pltpu.make_async_copy(ref, ref, hop_sem.at[kind, index]).wait()

    own_sums = pltpu.make_async_copy(
        slots_v.at[r], sums_out.at[:, pl.ds(pl.multiple_of(r * coarse, coarse), coarse), :], out_sem.at[3]
    )

    def send_sums():
        stash(r, c, dir_v)
        for y in range(nr):
            for s in range(own):
                g = jnp.clip(rb[y] + s, 0, grid_rows - 1)
                slots_v[y, s] = sums_g[g]
        row_peers(lambda y: send(
            slots_v.at[y], sums_out.at[:, pl.ds(pl.multiple_of(r * coarse, coarse), coarse), :], 10, (y, c)))
        own_sums.start()

    if nr == 8 and grid_rows % 2 == 0:
        near = r + 1 - 2 * lax.rem(r, 2)
        beside = r + 2 - 4 * lax.rem(r // 2, 2)
        across = r + 4 - 8 * lax.rem(r // 4, 2)
        far = beside + 4 - 8 * lax.rem(beside // 4, 2)
        order = [lax.rem(c + k, nc) for k in range(nc)]
        if nc == 4:
            upper = lax.div(c, 2)
            inner = c + upper * (3 - 2 * c)
            order = [c] + [z + upper * (3 - 2 * z) for z in (1 - inner, 2, 3)]
        for z in order[1:]:
            hop(piece(r, c), 0, c, (r, z), dir_v)

        def spread(z, src=None):
            hop(piece(r, z), 1, z, (beside, c), src)
            hop(piece(r, z), 2, z, (across, c), src)
            hop(piece(r, z), 5, z, (near, c), src)

        def relay(z):
            landed(piece(beside, z), 1, z)
            hop(piece(beside, z, 0), 3, z, (across, c))
            hop(piece(beside, z), 6, z, (near, c))
            landed(piece(across, z), 2, z)
            hop(piece(across, z, 1), 4, z, (beside, c))
            hop(piece(across, z), 7, z, (near, c))
            stash(beside, z)
            stash(across, z)

        def finish(z):
            landed(piece(far, z, 0), 3, z)
            landed(piece(far, z, 1), 4, z)
            hop(piece(far, z), 8, z, (near, c))
            stash(far, z)

        for k in range(nc + 2):
            if k < nc:
                z = order[k]
                if k:
                    landed(piece(r, z), 0, z)
                spread(z, None if k else dir_v)
                if k == 0:
                    send_sums()
                else:
                    stash(r, z)
            if 1 <= k < nc + 1:
                relay(order[k - 1])
            if k >= 2:
                finish(order[k - 2])
        nears = (near, near + 2 - 4 * lax.rem(near // 2, 2))
        nears = nears + tuple(v + 4 - 8 * lax.rem(v // 4, 2) for v in nears)
        for z in order:
            for kind, dev_row in enumerate(nears):
                landed(piece(dev_row, z), 5 + kind, z)
                stash(dev_row, z)
    else:
        others(lambda to, where: hop(piece(r, c), 0, 0, where, dir_v))
        send_sums()
        landed(around_v.at[pl.ds(0, n - 1)], 0, 0)
        others(lambda to, where: stash(*where))

    bytes_of(slots_v.at[pl.ds(0, nr - 1)], 11)
    for i, ref in (
        (0, ids.at[pl.ds(0, nc - 1)]), (2, send1.at[pl.ds(0, (n - 1) * pad)]),
        (4, send2.at[pl.ds(0, (nc - 1) * band_rows)]), (6, ids.at[pl.ds(0, (nr - 1) * nc)]),
        (8, states.at[pl.ds(0, nr - 1)]), (10, slots_v.at[pl.ds(0, nr - 1)]),
    ):
        bytes_of(ref, i)
    sent = around_v.at[pl.ds(0, n - 1)]
    pltpu.make_async_copy(sent, sent, hop_send).wait()
    stashed = pltpu.make_async_copy(around_v, around, out_sem.at[2])
    for copy in (keep, count_store, own_sums, stashed):
        copy.wait()


def place(
    nr, nc, cb_hbm, error_in, sums, counts, around, master, moment1, moment2,
    error_out, master_out, moment1_out, moment2_out, step_out,
    cb, err_v, state, sums_v, counts_v, step_v, in_sem, out_sem, step_sem,
):
    blocks, own, side = error_in.shape[0], master.shape[0], master.shape[1]
    grid_cols = nc - nc // 4
    coarse = side // nr
    pieces = 4
    part = blocks // pieces
    cuts = [pl.ds(i * part, part) for i in range(pieces)]
    ins = [pltpu.make_async_copy(error_in.at[cut], err_v.at[cut], in_sem.at[i]) for i, cut in enumerate(cuts)]
    outs = [pltpu.make_async_copy(err_v.at[cut], error_out.at[cut], out_sem.at[i]) for i, cut in enumerate(cuts)]
    small = [
        pltpu.make_async_copy(a, b, in_sem.at[pieces + i])
        for i, (a, b) in enumerate((
            (master, state.at[0]), (moment1, state.at[1]), (moment2, state.at[2]),
            (sums, sums_v), (counts, counts_v), (cb_hbm, cb),
        ))
    ]
    back = [
        pltpu.make_async_copy(state.at[i], b, out_sem.at[pieces + i])
        for i, b in enumerate((master_out, moment1_out, moment2_out))
    ]
    for copy in small[-1:] + ins + small[:-1]:
        copy.start()
    small[-1].wait()
    for col in range(grid_cols):
        band = band_of(cb, nc, col)
        for y in range(nr):
            pltpu.make_async_copy(
                around.at[y * nc + band], step_v.at[:, col, pl.ds(y * coarse, coarse), :], step_sem.at[col]
            ).start()
    for copy, then in zip(ins, outs):
        copy.wait()
        then.start()
    steps = []
    for col in range(grid_cols):
        pltpu.make_async_copy(step_v.at[:, col], step_v.at[:, col], step_sem.at[col]).wait()
        steps.append(pltpu.make_async_copy(step_v.at[:, col], step_out.at[:, col], step_sem.at[grid_cols + col]))
        steps[-1].start()
    for copy in small[:-1]:
        copy.wait()
    for s in range(own):
        changed = jnp.broadcast_to(counts_v[s:s + 1, :], (side, 128)) > 0.5
        old = [state[i, s] for i in range(3)]
        fresh = update(sums_v[s], *old, nr * nc)
        for i in range(3):
            state[i, s] = jnp.where(changed, fresh[i], old[i])
    for copy in back:
        copy.start()
    for copy in outs + back + steps:
        copy.wait()


def solution(mesh):
    nr, nc = mesh.shape["row"], mesh.shape["col"]
    n = nr * nc

    def local(grad, error, sel_blocks, row_bounds, col_bounds, master, moment1, moment2):
        blocks, side, _ = grad.shape
        picks, own = sel_blocks.shape[1], master.shape[0]
        rows, coarse = side // n, side // nr
        grid_cols = nc - nc // 4
        grid_rows = blocks // grid_cols
        pad = -(-picks * rows // 8) * 8
        f32, bf16, i32 = jnp.float32, jnp.bfloat16, jnp.int32
        anywhere = pl.BlockSpec(memory_space=pl.ANY)
        slots = jax.ShapeDtypeStruct(master.shape, f32)
        dma = pltpu.SemaphoreType.DMA
        new_error, sums, counts, around = pl.pallas_call(
            functools.partial(kernel, nr, nc, rows, pad),
            out_shape=(
                jax.ShapeDtypeStruct(error.shape, f32), slots,
                jax.ShapeDtypeStruct((8, 128), f32),
                jax.ShapeDtypeStruct((n, grid_rows, coarse, side), bf16),
            ),
            in_specs=[anywhere] * 8,
            out_specs=[anywhere] * 4,
            scratch_shapes=[
                pltpu.SMEM(sel_blocks.shape, i32),
                pltpu.SMEM(row_bounds.shape, i32),
                pltpu.SMEM(col_bounds.shape, i32),
                pltpu.VMEM(grad.shape, bf16),
                pltpu.VMEM(error.shape, f32),
                pltpu.VMEM((3,) + master.shape, f32),
                pltpu.VMEM((nr, 3, own, coarse, side), f32),
                pltpu.VMEM((side, side), f32),
                pltpu.VMEM((1, 128), i32),
                pltpu.VMEM((n, 1, 128), i32),
                pltpu.VMEM((n * pad, side), f32),
                pltpu.VMEM((n * pad, side), f32),
                pltpu.VMEM((nc * grid_rows * rows, side), f32),
                pltpu.VMEM((nc * grid_rows * rows, side), f32),
                pltpu.VMEM((grid_rows * coarse, side), f32),
                pltpu.VMEM((grid_rows, coarse, side), f32),
                pltpu.VMEM((nr, own, coarse, side), f32),
                pltpu.VMEM((8, 128), f32),
                pltpu.VMEM((grid_rows, coarse, side), bf16),
                pltpu.VMEM((n, grid_rows, coarse, side), bf16),
                dma((8,)), dma((4,)), dma((12,)), dma((9, nc)), dma,
            ],
            compiler_params=pltpu.CompilerParams(
                collective_id=0, has_side_effects=True, vmem_limit_bytes=64 * 1024 * 1024
            ),
        )(sel_blocks, row_bounds, col_bounds, grad, error, master, moment1, moment2)
        outs = pl.pallas_call(
            functools.partial(place, nr, nc),
            out_shape=(
                jax.ShapeDtypeStruct(error.shape, f32), slots, slots, slots,
                jax.ShapeDtypeStruct((grid_rows, grid_cols, side, side), bf16),
            ),
            in_specs=[anywhere] * 8,
            out_specs=[anywhere] * 5,
            scratch_shapes=[
                pltpu.SMEM(col_bounds.shape, i32),
                pltpu.VMEM(error.shape, f32),
                pltpu.VMEM((3,) + master.shape, f32),
                pltpu.VMEM(master.shape, f32),
                pltpu.VMEM((8, 128), f32),
                pltpu.VMEM((grid_rows, grid_cols, side, side), bf16),
                dma((10,)), dma((7,)), dma((2 * grid_cols,)),
            ],
            compiler_params=pltpu.CompilerParams(vmem_limit_bytes=64 * 1024 * 1024),
        )(col_bounds, new_error, sums, counts, around, master, moment1, moment2)
        return outs[:4] + (outs[4].reshape(grad.shape),)

    whole = P(("row", "col"), None, None)
    return jax.shard_map(
        local,
        mesh=mesh,
        in_specs=(whole, whole, P(("row", "col"), None), P(), P(), whole, whole, whole),
        out_specs=(whole, whole, whole, whole, P()),
        check_vma=False,
    )
```

```python
import functools

import jax
import jax.numpy as jnp
from jax import lax
from jax.experimental import pallas as pl
from jax.experimental.pallas import tpu as pltpu
from jax.sharding import PartitionSpec as P

CMAX = 1
BETA_ONE = 0.9
BETA_TWO = 0.95
EPSILON = 1e-08
DECAY_RATE = 0.1
LEARN_RATE = 0.01
CORRECT_ONE = 1.0 - 0.9**10
CORRECT_TWO = 1.0 - 0.95**10
MESH = pl.DeviceIdType.MESH


def rows_of(start, size, stride):
    return pl.ds(start, size) if stride == 1 else pl.ds(start, size, stride=stride)


def update(totals, master, moment1, moment2, n):
    averaged = totals / n
    first = BETA_ONE * moment1 + (1.0 - BETA_ONE) * averaged
    second = BETA_TWO * moment2 + (1.0 - BETA_TWO) * averaged * averaged
    direction = (
        first / CORRECT_ONE / (jnp.sqrt(second / CORRECT_TWO) + EPSILON) + DECAY_RATE * master
    )
    return (master - LEARN_RATE * direction, first, second, direction)


def band_of(bounds, bands, position):
    band = jnp.int32(0)
    for i in range(1, bands):
        band += (bounds[i] <= position).astype(jnp.int32)
    return band


def kernel(
    nr, nc, rows, pad,
    sel_hbm, rb_hbm, cb_hbm, grad, error, master, moment1, moment2,
    error_out, sums_out, counts_out, around,
    sel, rb, cb, grad_v, err_v, state, states, acc_v, id_mine, ids, send1, recv1,
    send2, recv2, sums_v, sums_g, slots_v, counts_v, dir_v, around_v,
    local_sem, out_sem, many_sem, hop_sem, hop_send,
):
    n = nr * nc
    blocks, side = grad.shape[0], grad.shape[1]
    picks, own = sel.shape[1], master.shape[0]
    grid_cols = nc - nc // 4
    grid_rows = blocks // grid_cols
    coarse = rows * nc
    band_rows = grid_rows * rows
    r, c = lax.axis_index("row"), lax.axis_index("col")
    me = r * nc + c

    def others(body):
        def step(k, carry):
            to = lax.rem(me + k, n)
            body(to, (lax.div(to, nc), lax.rem(to, nc)))
            return carry
        lax.fori_loop(1, n, step, 0, unroll=n <= 32)

    def send(src, dst, kind, where):
        pltpu.make_async_remote_copy(
            src_ref=src, dst_ref=dst, send_sem=many_sem.at[kind], recv_sem=many_sem.at[kind + 1],
            device_id=where, device_id_type=MESH,
        ).start()

    def row_peers(body):
        for k in range(1, nr):
            body(lax.rem(r + k, nr))

    def col_peers(body):
        for k in range(1, nc):
            body(lax.rem(c + k, nc))

    def bytes_of(ref, index):
        pltpu.make_async_copy(ref, ref, many_sem.at[index]).wait()

    barrier = pltpu.get_barrier_semaphore()
    loads = [
        pltpu.make_async_copy(a, b, local_sem.at[i])
        for i, (a, b) in enumerate(
            (
                (sel_hbm, sel), (rb_hbm, rb), (cb_hbm, cb), (grad, grad_v), (error, err_v),
                (master, state.at[0]), (moment1, state.at[1]), (moment2, state.at[2]),
            )
        )
    ]
    for load in loads:
        load.start()
    others(lambda to, where: pl.semaphore_signal(barrier, inc=1, device_id=where, device_id_type=MESH))
    for load in loads[:3]:
        load.wait()

    lane = lax.broadcasted_iota(jnp.int32, (1, 128), 1)
    part = lane % pad
    mine = jnp.full((1, 128), -1, jnp.int32)
    for s in range(picks):
        mine = jnp.where(part // rows == s, sel[0, s] * rows + part % rows, mine)
    id_mine[...] = mine
    ids[pl.ds(me, 1)] = mine[None]

    loads[3].wait()
    loads[4].wait()
    if pad > picks * rows:
        send1[...] = jnp.zeros_like(send1)
    for s in range(picks):
        pick = jnp.clip(sel[0, s], 0, blocks - 1)
        acc_v[...] = grad_v[pick].astype(jnp.float32) + err_v[pick]
        for q in range(rows):
            send1[rows_of(s * rows + q, n, pad), :] = acc_v[rows_of(q, n, rows), :]
    here = pl.ds(pl.multiple_of(me * pad, pad), pad)
    recv1[here, :] = send1[here, :]

    pl.semaphore_wait(barrier, n - 1)
    col_peers(lambda z: send(id_mine, ids.at[me], 0, (r, z)))
    others(lambda to, where: send(
        send1.at[pl.ds(pl.multiple_of(to * pad, pad), pad)], recv1.at[here], 2, where))
    bytes_of(ids.at[pl.ds(0, nc - 1)], 1)
    line = ids.at[pl.ds(r * nc, nc)]
    row_peers(lambda y: send(line, line, 6, (y, c)))

    for load in loads[5:]:
        load.wait()
    row_peers(lambda y: send(
        state.at[:, :, pl.ds(pl.multiple_of(y * coarse, coarse), coarse), :], states.at[r], 8, (y, c)))
    states[r] = state[:, :, pl.ds(pl.multiple_of(r * coarse, coarse), coarse), :]

    bytes_of(ids.at[pl.ds(0, (nr - 1) * nc)], 7)
    per = 128 // pad
    tiles = []
    for j in range(n * pad // 128):
        tile = jnp.zeros((1, 128), jnp.int32)
        for k in range(per):
            tile = jnp.where(lane // pad == k, ids[j * per + k], tile)
        tiles.append(tile)

    def table_of(wanted):
        return [(wanted == tile).astype(jnp.float32) for tile in tiles]

    def tally(wanted):
        return jnp.sum(functools.reduce(jnp.add, table_of(wanted)), axis=1, keepdims=True)

    index = lax.broadcasted_iota(jnp.int32, (band_rows, 128), 0)
    table = []
    for band in range(nc):
        column = jnp.full((band_rows, 128), cb[band], jnp.int32)
        wanted = (index // rows * grid_cols + column) * rows + index % rows
        wanted = jnp.where(column < cb[band + 1], wanted, -2)
        table.append(jnp.concatenate(table_of(wanted), axis=1))
    table = jnp.concatenate(table, axis=0).astype(jnp.bfloat16)

    bytes_of(recv1.at[pl.ds(0, (n - 1) * pad)], 3)
    got = recv1[...]
    high = got.astype(jnp.bfloat16)
    rest = got - high.astype(jnp.float32)
    middle = rest.astype(jnp.bfloat16)
    low = (rest - middle.astype(jnp.float32)).astype(jnp.bfloat16)
    dot = functools.partial(jnp.dot, preferred_element_type=jnp.float32)
    send2[...] = dot(table, high) + (dot(table, middle) + dot(table, low))
    band_here = pl.ds(pl.multiple_of(c * band_rows, 8), band_rows)
    col_peers(lambda z: send(
        send2.at[pl.ds(pl.multiple_of(z * band_rows, 8), band_rows)], recv2.at[band_here], 4, (r, z)))
    recv2[band_here, :] = send2[band_here, :]

    index = lax.broadcasted_iota(jnp.int32, (grid_rows * coarse, 128), 0)
    column = jnp.full((grid_rows * coarse, 128), cb[c], jnp.int32)
    wanted = jnp.where(column < cb[c + 1], (index // coarse * grid_cols + column) * rows, -2)
    counts = tally(wanted)
    slot = lax.broadcasted_iota(jnp.int32, (8, 128), 0)
    column = jnp.full((8, 128), cb[c], jnp.int32)
    inside = (column < cb[c + 1]) & (slot < own) & (rb[r] + slot < rb[r + 1])
    wanted = jnp.where(inside, ((rb[r] + slot) * grid_cols + column) * rows, -2)
    counts_v[...] = jnp.broadcast_to(tally(wanted), (8, 128))
    count_store = pltpu.make_async_copy(counts_v, counts_out, out_sem.at[1])
    count_store.start()

    def clear(b, carry):
        chosen = (sel[0, 0] == b).astype(jnp.float32)
        for s in range(1, picks):
            chosen += (sel[0, s] == b).astype(jnp.float32)
        err_v[b] = (grad_v[b].astype(jnp.float32) + err_v[b]) * (1.0 - chosen)
        return carry

    lax.fori_loop(0, blocks, clear, 0)
    keep = pltpu.make_async_copy(err_v, error_out, out_sem.at[0])
    keep.start()

    bytes_of(states.at[pl.ds(0, nr - 1)], 9)
    bytes_of(recv2.at[pl.ds(0, (nc - 1) * band_rows)], 5)

    for z in range(nc):
        for q in range(rows):
            sums_v[rows_of(z * rows + q, grid_rows, coarse), :] = recv2[
                rows_of(z * band_rows + q, grid_rows, rows), :]
    for g in range(grid_rows):
        band = band_of(rb, nr, g)
        offset = jnp.clip(g - rb[band], 0, own - 1)
        span = slice(g * coarse, (g + 1) * coarse)
        changed = jnp.broadcast_to(counts[span, :], (coarse, side)) > 0.5
        sums_g[g] = sums_v[span, :]
        direction = update(
            sums_v[span, :], states[band, 0, offset], states[band, 1, offset], states[band, 2, offset], n
        )[3]
        dir_v[g] = jnp.where(changed, direction, 0.0).astype(jnp.bfloat16)

    half = grid_rows // 2

    def piece(dev_row, dev_col, part=None):
        if part is None:
            return around_v.at[dev_row * nc + dev_col]
        return around_v.at[dev_row * nc + dev_col, pl.ds(part * half, half)]

    def stash(dev_row, dev_col, src=None):
        pltpu.make_async_copy(
            piece(dev_row, dev_col) if src is None else src, around.at[dev_row * nc + dev_col], out_sem.at[2]
        ).start()

    def hop(ref, kind, index, where, src=None):
        pltpu.make_async_remote_copy(
            src_ref=ref if src is None else src, dst_ref=ref, send_sem=hop_send,
            recv_sem=hop_sem.at[kind, index], device_id=where, device_id_type=MESH,
        ).start()

    def landed(ref, kind, index):
        pltpu.make_async_copy(ref, ref, hop_sem.at[kind, index]).wait()

    own_sums = pltpu.make_async_copy(
        slots_v.at[r], sums_out.at[:, pl.ds(pl.multiple_of(r * coarse, coarse), coarse), :], out_sem.at[3]
    )

    def send_sums():
        stash(r, c, dir_v)
        for y in range(nr):
            for s in range(own):
                g = jnp.clip(rb[y] + s, 0, grid_rows - 1)
                slots_v[y, s] = sums_g[g]
        row_peers(lambda y: send(
            slots_v.at[y], sums_out.at[:, pl.ds(pl.multiple_of(r * coarse, coarse), coarse), :], 10, (y, c)))
        own_sums.start()

    if nr == 8 and grid_rows % 2 == 0:
        near = r + 1 - 2 * lax.rem(r, 2)
        beside = r + 2 - 4 * lax.rem(r // 2, 2)
        across = r + 4 - 8 * lax.rem(r // 4, 2)
        far = beside + 4 - 8 * lax.rem(beside // 4, 2)
        order = [lax.rem(c + k, nc) for k in range(nc)]
        if nc == 4:
            upper = lax.div(c, 2)
            inner = c + upper * (3 - 2 * c)
            order = [c] + [z + upper * (3 - 2 * z) for z in (1 - inner, 2, 3)]
        for z in order[1:]:
            hop(piece(r, c), 0, c, (r, z), dir_v)

        def spread(z, src=None, direct=False):
            if direct:
                hop(piece(r, z), 3, z, (far, c), src)
            hop(piece(r, z), 1, z, (beside, c), src)
            hop(piece(r, z), 2, z, (across, c), src)
            hop(piece(r, z), 5, z, (near, c), src)

        def relay(z, direct):
            landed(piece(beside, z), 1, z)
            if not direct:
                hop(piece(beside, z, 0), 3, z, (across, c))
            hop(piece(beside, z), 6, z, (near, c))
            landed(piece(across, z), 2, z)
            if not direct:
                hop(piece(across, z, 1), 4, z, (beside, c))
            hop(piece(across, z), 7, z, (near, c))
            stash(beside, z)
            stash(across, z)

        def finish(z, direct):
            if direct:
                landed(piece(far, z), 3, z)
            else:
                landed(piece(far, z, 0), 3, z)
                landed(piece(far, z, 1), 4, z)
            hop(piece(far, z), 8, z, (near, c))
            stash(far, z)

        for k in range(nc + 2):
            if k < nc:
                z = order[k]
                if k:
                    landed(piece(r, z), 0, z)
                spread(z, None if k else dir_v, k == nc - 1)
                if k == 0:
                    send_sums()
                else:
                    stash(r, z)
            if 1 <= k < nc + 1:
                relay(order[k - 1], k == nc)
            if k >= 2:
                finish(order[k - 2], k == nc + 1)
        nears = (near, near + 2 - 4 * lax.rem(near // 2, 2))
        nears = nears + tuple(v + 4 - 8 * lax.rem(v // 4, 2) for v in nears)
        for z in order:
            for kind, dev_row in enumerate(nears):
                landed(piece(dev_row, z), 5 + kind, z)
                stash(dev_row, z)
    else:
        others(lambda to, where: hop(piece(r, c), 0, 0, where, dir_v))
        send_sums()
        landed(around_v.at[pl.ds(0, n - 1)], 0, 0)
        others(lambda to, where: stash(*where))

    bytes_of(slots_v.at[pl.ds(0, nr - 1)], 11)
    for i, ref in (
        (0, ids.at[pl.ds(0, nc - 1)]), (2, send1.at[pl.ds(0, (n - 1) * pad)]),
        (4, send2.at[pl.ds(0, (nc - 1) * band_rows)]), (6, ids.at[pl.ds(0, (nr - 1) * nc)]),
        (8, states.at[pl.ds(0, nr - 1)]), (10, slots_v.at[pl.ds(0, nr - 1)]),
    ):
        bytes_of(ref, i)
    sent = around_v.at[pl.ds(0, n - 1)]
    pltpu.make_async_copy(sent, sent, hop_send).wait()
    stashed = pltpu.make_async_copy(around_v, around, out_sem.at[2])
    for copy in (keep, count_store, own_sums, stashed):
        copy.wait()


def place(
    nr, nc, cb_hbm, error_in, sums, counts, around, master, moment1, moment2,
    error_out, master_out, moment1_out, moment2_out, step_out,
    cb, err_v, state, sums_v, counts_v, step_v, in_sem, out_sem, step_sem,
):
    blocks, own, side = error_in.shape[0], master.shape[0], master.shape[1]
    grid_cols = nc - nc // 4
    coarse = side // nr
    pieces = 4
    part = blocks // pieces
    cuts = [pl.ds(i * part, part) for i in range(pieces)]
    ins = [pltpu.make_async_copy(error_in.at[cut], err_v.at[cut], in_sem.at[i]) for i, cut in enumerate(cuts)]
    outs = [pltpu.make_async_copy(err_v.at[cut], error_out.at[cut], out_sem.at[i]) for i, cut in enumerate(cuts)]
    small = [
        pltpu.make_async_copy(a, b, in_sem.at[pieces + i])
        for i, (a, b) in enumerate((
            (master, state.at[0]), (moment1, state.at[1]), (moment2, state.at[2]),
            (sums, sums_v), (counts, counts_v), (cb_hbm, cb),
        ))
    ]
    back = [
        pltpu.make_async_copy(state.at[i], b, out_sem.at[pieces + i])
        for i, b in enumerate((master_out, moment1_out, moment2_out))
    ]
    for copy in small[-1:] + ins + small[:-1]:
        copy.start()
    small[-1].wait()
    for col in range(grid_cols):
        band = band_of(cb, nc, col)
        for y in range(nr):
            pltpu.make_async_copy(
                around.at[y * nc + band], step_v.at[:, col, pl.ds(y * coarse, coarse), :], step_sem.at[col]
            ).start()
    for copy, then in zip(ins, outs):
        copy.wait()
        then.start()
    steps = []
    for col in range(grid_cols):
        pltpu.make_async_copy(step_v.at[:, col], step_v.at[:, col], step_sem.at[col]).wait()
        steps.append(pltpu.make_async_copy(step_v.at[:, col], step_out.at[:, col], step_sem.at[grid_cols + col]))
        steps[-1].start()
    for copy in small[:-1]:
        copy.wait()
    for s in range(own):
        changed = jnp.broadcast_to(counts_v[s:s + 1, :], (side, 128)) > 0.5
        old = [state[i, s] for i in range(3)]
        fresh = update(sums_v[s], *old, nr * nc)
        for i in range(3):
            state[i, s] = jnp.where(changed, fresh[i], old[i])
    for copy in back:
        copy.start()
    for copy in outs + back + steps:
        copy.wait()


def solution(mesh):
    nr, nc = mesh.shape["row"], mesh.shape["col"]
    n = nr * nc

    def local(grad, error, sel_blocks, row_bounds, col_bounds, master, moment1, moment2):
        blocks, side, _ = grad.shape
        picks, own = sel_blocks.shape[1], master.shape[0]
        rows, coarse = side // n, side // nr
        grid_cols = nc - nc // 4
        grid_rows = blocks // grid_cols
        pad = -(-picks * rows // 8) * 8
        f32, bf16, i32 = jnp.float32, jnp.bfloat16, jnp.int32
        anywhere = pl.BlockSpec(memory_space=pl.ANY)
        slots = jax.ShapeDtypeStruct(master.shape, f32)
        dma = pltpu.SemaphoreType.DMA
        new_error, sums, counts, around = pl.pallas_call(
            functools.partial(kernel, nr, nc, rows, pad),
            out_shape=(
                jax.ShapeDtypeStruct(error.shape, f32), slots,
                jax.ShapeDtypeStruct((8, 128), f32),
                jax.ShapeDtypeStruct((n, grid_rows, coarse, side), bf16),
            ),
            in_specs=[anywhere] * 8,
            out_specs=[anywhere] * 4,
            scratch_shapes=[
                pltpu.SMEM(sel_blocks.shape, i32),
                pltpu.SMEM(row_bounds.shape, i32),
                pltpu.SMEM(col_bounds.shape, i32),
                pltpu.VMEM(grad.shape, bf16),
                pltpu.VMEM(error.shape, f32),
                pltpu.VMEM((3,) + master.shape, f32),
                pltpu.VMEM((nr, 3, own, coarse, side), f32),
                pltpu.VMEM((side, side), f32),
                pltpu.VMEM((1, 128), i32),
                pltpu.VMEM((n, 1, 128), i32),
                pltpu.VMEM((n * pad, side), f32),
                pltpu.VMEM((n * pad, side), f32),
                pltpu.VMEM((nc * grid_rows * rows, side), f32),
                pltpu.VMEM((nc * grid_rows * rows, side), f32),
                pltpu.VMEM((grid_rows * coarse, side), f32),
                pltpu.VMEM((grid_rows, coarse, side), f32),
                pltpu.VMEM((nr, own, coarse, side), f32),
                pltpu.VMEM((8, 128), f32),
                pltpu.VMEM((grid_rows, coarse, side), bf16),
                pltpu.VMEM((n, grid_rows, coarse, side), bf16),
                dma((8,)), dma((4,)), dma((12,)), dma((9, nc)), dma,
            ],
            compiler_params=pltpu.CompilerParams(
                collective_id=0, has_side_effects=True, vmem_limit_bytes=64 * 1024 * 1024
            ),
        )(sel_blocks, row_bounds, col_bounds, grad, error, master, moment1, moment2)
        outs = pl.pallas_call(
            functools.partial(place, nr, nc),
            out_shape=(
                jax.ShapeDtypeStruct(error.shape, f32), slots, slots, slots,
                jax.ShapeDtypeStruct((grid_rows, grid_cols, side, side), bf16),
            ),
            in_specs=[anywhere] * 8,
            out_specs=[anywhere] * 5,
            scratch_shapes=[
                pltpu.SMEM(col_bounds.shape, i32),
                pltpu.VMEM(error.shape, f32),
                pltpu.VMEM((3,) + master.shape, f32),
                pltpu.VMEM(master.shape, f32),
                pltpu.VMEM((8, 128), f32),
                pltpu.VMEM((grid_rows, grid_cols, side, side), bf16),
                dma((10,)), dma((7,)), dma((2 * grid_cols,)),
            ],
            compiler_params=pltpu.CompilerParams(vmem_limit_bytes=64 * 1024 * 1024),
        )(col_bounds, new_error, sums, counts, around, master, moment1, moment2)
        return outs[:4] + (outs[4].reshape(grad.shape),)

    whole = P(("row", "col"), None, None)
    return jax.shard_map(
        local,
        mesh=mesh,
        in_specs=(whole, whole, P(("row", "col"), None), P(), P(), whole, whole, whole),
        out_specs=(whole, whole, whole, whole, P()),
        check_vma=False,
    )
```
